512 devices in a mesh: seq: 64 (over z, x), head: 8 (over y, core).
Axes of the slice: x: 4, y: 4, z: 16, core: 2. Of those that a mesh axis runs over, the one named last changes fastest.
Arguments:
- hidden_in: bfloat16 [8192, 2048], P(('seq', 'head')), may hold values from -6 to 6
- w_inner: bfloat16 [2048, 4096], P(None, 'head'), may hold values from -0.125 to 0.125
- w_inout: bfloat16 [2048, 512], replicated, may hold values from -0.00390625 to 0.00390625
- w_step: bfloat16 [2, 2048, 64], P(None, None, 'head'), may hold values from -0.125 to 0.125
- step_bias: float32 [2, 64], P(None, 'head'), may hold values from -1 to 1
- decay_rate: float32 [64], P('head'), may hold values from 2e-05 to 0.05
- skip_gain: float32 [64], P('head'), may hold values from 0.5 to 1.5
Outputs:
- mixed: bfloat16 [8192, 4096], P('seq', 'head')
The draws below stay inside these ranges and needn't reach their ends.
All inputs are finite; a program needn't handle non-finite values.
Results may differ from the reference program's by a relative error of at most 0.0052.
Values may be sent and summed in bfloat16 or wider, within the bound.
No kernel may reach another device: no remote copies, remote signals or barrier semaphores. Data moves between devices by JAX's collectives and lax.ppermute only.
A program may use at most 128 MiB of HBM per device.

```python
import math
import jax
import jax.numpy as jnp
from jax import lax

DMODEL = 2048
HEADS = 64
HEADDIM = 64
STATE = 128
SPAN = 128
DINNER = 4096
TOKENS = 8192


def steps_of(stream_key, shape, split, smallest, largest):
    loudness, own = 1.0, jax.random.fold_in(stream_key, 6)
    for dim, shards_of in split:
        steps = jnp.exp(jax.random.uniform(jax.random.fold_in(own, dim), (shards_of,), jnp.float32, smallest / len(split), largest / len(split)))
        loudness = loudness * jnp.repeat(steps, shape[dim] // shards_of).reshape([-1 if axis == dim else 1 for axis in range(len(shape))])
    return loudness


def normal_values(own_key, shape, scale, limit, cuts=(), dtype=jnp.bfloat16):
    result = jax.random.normal(own_key, shape, jnp.float32) * scale
    if len(cuts) > 0:
        result = steps_of(own_key, shape, cuts, -0.22, 0.18) * result
    return jnp.clip(result, min=-limit, max=limit).astype(dtype)


def setup_inputs(seed: int = 0) -> dict:
    key_of = jax.random.split(jax.random.key(seed), 8)
    return {
        "hidden_in": normal_values(key_of[0], (TOKENS, DMODEL), 1.0, 6.0, ((0, 512),)),
        "w_inner": normal_values(key_of[1], (DMODEL, DINNER), DMODEL ** -0.5, 0.125, ((1, 8),)),
        "w_inout": normal_values(key_of[2], (DMODEL, 4 * STATE), (DMODEL * TOKENS // 8) ** -0.5, 0.00390625),
        "w_step": normal_values(key_of[3], (2, DMODEL, HEADS), DMODEL ** -0.5, 0.125, ((2, 8),)),
        "step_bias": jnp.clip(jax.random.uniform(key_of[4], (2, HEADS), jnp.float32, -1.0, 1.0) * steps_of(key_of[4], (2, HEADS), ((1, 8),), -0.4, 0.0), -1.0, 1.0),
        "decay_rate": jnp.clip(jnp.exp(math.log(0.05) - 7.824046 * jax.random.uniform(key_of[5], (HEADS,), jnp.float32) ** steps_of(key_of[5], (HEADS,), ((0, 8),), -0.2, 0.2)), 1.9999999494757503e-05, 0.05),
        "skip_gain": jnp.clip(0.5 + 1.0 * jax.random.uniform(key_of[6], (HEADS,), jnp.float32) ** steps_of(key_of[6], (HEADS,), ((0, 8),), -0.2, 0.2), 0.5, 1.5),
    }


def span_pass(inner, in_map, out_map, steps, rate):
    rows, heads_here, width = inner.shape
    count = rows // SPAN
    states = in_map.shape[1]
    exact = lax.Precision.HIGHEST
    values = inner.astype(jnp.float32).reshape(count, SPAN, heads_here, width)
    in_blocks = in_map.astype(jnp.float32).reshape(count, SPAN, states)
    out_blocks = out_map.astype(jnp.float32).reshape(count, SPAN, states)
    logs = (-steps * rate[None, :]).reshape(count, SPAN, heads_here).transpose(0, 2, 1)
    step_blocks = steps.reshape(count, SPAN, heads_here).transpose(0, 2, 1)
    cums = jnp.cumsum(logs, axis=2)
    scores = jnp.einsum('kin,kjn->kij', out_blocks, in_blocks, precision=exact)
    spread = cums[:, :, :, None] - cums[:, :, None, :]
    lower = jnp.arange(SPAN)[:, None] > jnp.arange(SPAN)[None, :]
    decay = jnp.where(lower, jnp.exp(jnp.where(lower, spread, 0.0)), 0.0)
    weights = decay * scores[:, None, :, :] * step_blocks[:, :, None, :]
    intra = jnp.einsum('khij,kjhp->kihp', weights, values, precision=exact)
    tail = jnp.exp(cums[:, :, -1:] - cums) * step_blocks
    pieces = jnp.einsum('khj,kjn,kjhp->khnp', tail, in_blocks, values, precision=exact)
    totals = cums[:, :, -1]

    def advance(carry, item):
        total, piece = item
        return jnp.exp(total)[:, None, None] * carry + piece, carry

    last, starts = lax.scan(advance, jnp.zeros((heads_here, states, width), jnp.float32), (totals, pieces))
    inter = jnp.einsum('khi,kin,khnp->kihp', jnp.exp(cums), out_blocks, starts, precision=exact)
    return (intra + inter).reshape(rows, heads_here, width), last


def reference(hidden_in, w_inner, w_inout, w_step, step_bias, decay_rate, skip_gain):
    inner = jnp.dot(hidden_in, w_inner, preferred_element_type=jnp.float32).astype(jnp.bfloat16)
    inner = inner.reshape(TOKENS, HEADS, HEADDIM)
    maps = jnp.dot(hidden_in, w_inout, preferred_element_type=jnp.float32).astype(jnp.bfloat16)
    in_fwd = maps[:, :STATE]
    out_fwd = maps[:, STATE:2 * STATE]
    in_bwd = maps[:, 2 * STATE:3 * STATE]
    out_bwd = maps[:, 3 * STATE:]
    step_fwd = jax.nn.softplus(jnp.dot(hidden_in, w_step[0], preferred_element_type=jnp.float32) + step_bias[0][None, :])
    step_bwd = jax.nn.softplus(jnp.dot(hidden_in, w_step[1], preferred_element_type=jnp.float32) + step_bias[1][None, :])

    def per_head(item):
        values, forward_steps, backward_steps, rate = item
        ahead = span_pass(values, in_fwd, out_fwd, forward_steps, rate)[0]
        behind = span_pass(jnp.flip(values, 0), jnp.flip(in_bwd, 0), jnp.flip(out_bwd, 0), jnp.flip(backward_steps, 0), rate)[0]
        return ahead + jnp.flip(behind, 0)

    mixed = lax.map(per_head, (inner.transpose(1, 0, 2)[:, :, None, :], step_fwd.T[:, :, None], step_bwd.T[:, :, None], decay_rate[:, None]))
    mixed = mixed[:, :, 0, :].transpose(1, 0, 2)
    mixed = mixed + skip_gain[None, :, None] * inner.astype(jnp.float32)
    return mixed.reshape(TOKENS, DINNER).astype(jnp.bfloat16)
```

```python
import jax
import jax.numpy as jnp
from jax import lax
from jax.experimental import pallas as pl
from jax.experimental.pallas import tpu as pltpu
from jax.sharding import PartitionSpec as P

SPAN = 128
HEADDIM = 64
STATE = 128
EXTRA = 8
F32 = jnp.float32
BF16 = jnp.bfloat16
LAST = (((1,), (1,)), ((), ()))
FIRST = (((0,), (0,)), ((), ()))


def dot(a, b, dims=None, precision=None):
    dims = dims or (((1,), (0,)), ((), ()))
    return lax.dot_general(a, b, dims, precision=precision, preferred_element_type=F32)


def iota(shape, dim):
    return lax.broadcasted_iota(jnp.int32, shape, dim)


def local_kernel(x_ref, wi_ref, wm_ref, ws_ref, bias_ref, rate_ref, gain_ref, send_ref, y_ref, out_ref, reach_ref):
    owners = send_ref.shape[0]
    heads = rate_ref.shape[1] // 2
    share = heads * HEADDIM // owners
    x = x_ref[...]
    pre = dot(x, ws_ref[...], LAST) + bias_ref[...]
    step = jnp.maximum(pre, 0.0) + jnp.log1p(jnp.exp(-jnp.abs(pre)))
    logs = -rate_ref[...] * step
    row, col = iota((SPAN, SPAN), 0), iota((SPAN, SPAN), 1)
    lower, upper = row > col, row < col
    exact = lax.Precision.HIGHEST
    ahead = dot((row >= col).astype(F32), logs, precision=exact)
    behind = dot((row <= col).astype(F32), logs, precision=exact)
    forward = iota(logs.shape, 1) < heads
    cum = jnp.where(forward, ahead, behind)
    total = jnp.where(forward[:1], cum[SPAN - 1 :], cum[:1])
    tail = jnp.exp(total - cum) * step
    reach_ref[...] = jnp.exp(cum)
    decay = jnp.exp(total)
    cum_t, step_t = cum.T, step.T

    maps = dot(x, wm_ref[...]).astype(BF16)
    in_f, out_f = maps[:, :STATE], maps[:, STATE : 2 * STATE]
    in_b, out_b = maps[:, 2 * STATE : 3 * STATE], maps[:, 3 * STATE :]
    out_ref[:, :STATE] = out_f
    out_ref[:, STATE:] = out_b
    scores = jnp.where(lower, dot(out_f, in_f, LAST), jnp.where(upper, dot(out_b, in_b, LAST), 0.0))
    in_f32, in_b32 = in_f.astype(F32), in_b.astype(F32)
    inner = dot(x, wi_ref[...]).astype(BF16)
    mark = iota((EXTRA, STATE), 0)
    left = iota((SPAN, 2 * HEADDIM), 1) < HEADDIM
    zero = jnp.zeros((SPAN, 2 * HEADDIM), BF16)

    for pair in range(heads // 2):
        both = inner[:, 2 * HEADDIM * pair : 2 * HEADDIM * (pair + 1)]
        weights = []
        for h in (2 * pair, 2 * pair + 1):
            g = h + heads
            spread = jnp.where(
                lower,
                cum[:, h : h + 1] - cum_t[h : h + 1],
                cum[:, g : g + 1] - cum_t[g : g + 1],
            )
            steps = jnp.where(lower, step_t[h : h + 1], step_t[g : g + 1])
            weights.append((jnp.exp(spread) * (scores * steps)).astype(BF16))
            tailed = jnp.concatenate([in_f32 * tail[:, h : h + 1], in_b32 * tail[:, g : g + 1]], axis=1).astype(BF16)
            piece = dot(both[:, HEADDIM * (h % 2) : HEADDIM * (h % 2 + 1)], tailed, FIRST)
            piece = piece.reshape(HEADDIM // share, share, 2 * STATE)
            first = h * (HEADDIM // share)
            chunks = pl.ds(first, HEADDIM // share)
            rows = jnp.concatenate([piece[:, :, :STATE], piece[:, :, STATE:]], axis=1)
            send_ref[chunks, 0 : 2 * share, :] = rows.astype(BF16)
            d_f, d_b = decay[:, h : h + 1], decay[:, g : g + 1]
            high_f, high_b = d_f.astype(BF16).astype(F32), d_b.astype(BF16).astype(F32)
            marks = jnp.where(mark == 0, high_f, 0.0) + jnp.where(mark == 1, d_f - high_f, 0.0)
            marks = marks + jnp.where(mark == 2, high_b, 0.0) + jnp.where(mark == 3, d_b - high_b, 0.0)
            send_ref[chunks, 2 * share : 2 * share + EXTRA, :] = jnp.broadcast_to(
                marks[None], (HEADDIM // share, EXTRA, STATE)
            ).astype(BF16)
        stacked = jnp.concatenate([jnp.where(left, both, zero), jnp.where(left, zero, both)], axis=0)
        here = slice(2 * HEADDIM * pair, 2 * HEADDIM * (pair + 1))
        y_ref[:, here] = dot(jnp.concatenate(weights, axis=1), stacked) + gain_ref[:, here] * both.astype(F32)


def scan_kernel(got_ref, back_ref, held):
    blocks = got_ref.shape[0]
    share = back_ref.shape[1] // 2
    zero = jnp.zeros((share, STATE), F32)

    def one(step, carry):
        state_f, state_b = carry
        other = blocks - 1 - step
        held[step, :share] = state_f
        held[other, share:] = state_b
        here, there = got_ref[step].astype(F32), got_ref[other].astype(F32)
        d_f = here[2 * share : 2 * share + 1] + here[2 * share + 1 : 2 * share + 2]
        d_b = there[2 * share + 2 : 2 * share + 3] + there[2 * share + 3 : 2 * share + 4]
        return d_f * state_f + here[:share], d_b * state_b + there[share : 2 * share]

    lax.fori_loop(0, blocks, one, (zero, zero), unroll=4)
    back_ref[...] = held[...].astype(BF16)


def final_kernel(state_ref, out_ref, reach_ref, y_ref, mixed_ref):
    owners, rows, _ = state_ref.shape
    share = rows // 2
    heads = reach_ref.shape[1] // 2
    state = state_ref[...].astype(F32)
    ahead = state[:, :share].reshape(owners * share, STATE).astype(BF16)
    behind = state[:, share:].reshape(owners * share, STATE).astype(BF16)
    far_f = dot(out_ref[:, :STATE], ahead, LAST)
    far_b = dot(out_ref[:, STATE:], behind, LAST)
    reach = reach_ref[...]
    left = iota((SPAN, 2 * HEADDIM), 1) < HEADDIM
    for pair in range(heads // 2):
        here = slice(2 * HEADDIM * pair, 2 * HEADDIM * (pair + 1))
        h, g = 2 * pair, 2 * pair + heads
        scale_f = jnp.where(left, reach[:, h : h + 1], reach[:, h + 1 : h + 2])
        scale_b = jnp.where(left, reach[:, g : g + 1], reach[:, g + 1 : g + 2])
        mixed_ref[:, here] = (y_ref[:, here] + scale_f * far_f[:, here] + scale_b * far_b[:, here]).astype(BF16)


def call(kernel, out_shape, flops, scratch=()):
    return pl.pallas_call(
        kernel,
        out_shape=out_shape,
        scratch_shapes=list(scratch),
        compiler_params=pltpu.CompilerParams(vmem_limit_bytes=24 * 1024 * 1024),
        cost_estimate=pl.CostEstimate(flops=flops, bytes_accessed=1 << 20, transcendentals=0),
    )


def shards(hidden_in, w_inner, w_inout, w_step, step_bias, decay_rate, skip_gain):
    heads = w_step.shape[2]
    width = w_inner.shape[1]
    blocks = lax.axis_size("seq")
    share = width // blocks
    rows = 2 * share
    x = lax.all_gather(hidden_in, "head", axis=0, tiled=True)
    w_rows = w_step.transpose(0, 2, 1).reshape(2 * heads, -1)
    bias = step_bias.reshape(1, 2 * heads)
    rate = jnp.concatenate([decay_rate, decay_rate])[None, :]
    gain = jnp.repeat(skip_gain, HEADDIM)[None, :]
    shape = jax.ShapeDtypeStruct
    send, near, outs, reach = call(
        local_kernel,
        (
            shape((blocks, rows + EXTRA, STATE), BF16),
            shape((SPAN, width), F32),
            shape((SPAN, 2 * STATE), BF16),
            shape((SPAN, 2 * heads), F32),
        ),
        700_000_000,
    )(x, w_inner, w_inout, w_rows, bias, rate, gain)
    got = lax.all_to_all(send, "seq", 0, 0, tiled=True)
    back = call(
        scan_kernel,
        shape((blocks, rows, STATE), BF16),
        1_000_000,
        (pltpu.VMEM((blocks, rows, STATE), F32),),
    )(got)
    state = lax.all_to_all(back, "seq", 0, 0, tiled=True)
    return call(final_kernel, shape((SPAN, width), BF16), 40_000_000)(state, outs, reach, near)


def solution(mesh):
    placed = (
        P(("seq", "head"), None),
        P(None, "head"),
        P(),
        P(None, None, "head"),
        P(None, "head"),
        P("head"),
        P("head"),
    )
    return jax.shard_map(
        shards, mesh=mesh, in_specs=placed, out_specs=P("seq", "head"), check_vma=False
    )
```

```python
import jax
import jax.numpy as jnp
from jax import lax
from jax.experimental import pallas as pl
from jax.experimental.pallas import tpu as pltpu
from jax.sharding import Mesh, PartitionSpec as P

SPAN = 128
HEADDIM = 64
STATE = 128
EXTRA = 8
CUTS = 4
F32 = jnp.float32
BF16 = jnp.bfloat16
LAST = (((1,), (1,)), ((), ()))
FIRST = (((0,), (0,)), ((), ()))
VMEM = pl.BlockSpec(memory_space=pltpu.VMEM)
HBM = pl.BlockSpec(memory_space=pltpu.HBM)


def dot(a, b, dims=None, precision=None):
    dims = dims or (((1,), (0,)), ((), ()))
    return lax.dot_general(a, b, dims, precision=precision, preferred_element_type=F32)


def iota(shape, dim):
    return lax.broadcasted_iota(jnp.int32, shape, dim)


def split(value, first):
    mark = iota((EXTRA, STATE), 0)
    high = value.astype(BF16).astype(F32)
    return jnp.where(mark == first, high, 0.0) + jnp.where(mark == first + 1, value - high, 0.0)


def joined(rows, first):
    return rows[first : first + 1] + rows[first + 1 : first + 2]


def fetch(pairs, sems):
    waits, used = [], 0
    for src, dst in pairs:
        cuts = CUTS if src.shape[0] % (16 * CUTS) == 0 else 1
        size = src.shape[0] // cuts
        copies = []
        for cut in range(cuts):
            part = pl.ds(cut * size, size)
            ends = (src.at[part], dst.at[part]) if cuts > 1 else (src, dst)
            copies.append(pltpu.make_async_copy(*ends, sems.at[used + cut]))
        used += cuts
        for copy in copies:
            copy.start()
        waits.append(copies)
    return waits


def ready(copies):
    for copy in copies:
        copy.wait()


def local_kernel(mine_ref, other_ref, *refs):
    ws_ref, small_ref, *sources = refs[:4]
    send_ref, y_ref, out_ref, reach_ref = refs[4:8]
    wm_ref, wi_ref = held = refs[8:10]
    sems = refs[10]
    waits = fetch(zip(sources, held), sems)
    heads = send_ref.shape[0]
    first = lax.axis_index("core") == 0
    parts = []
    for y in range(mine_ref.shape[0]):
        mine, other = mine_ref[y], other_ref[y]
        parts += [jnp.where(first, mine, other), jnp.where(first, other, mine)]
    x = jnp.concatenate(parts, axis=0)
    bias_f, bias_b, rate, gain = (small_ref[row : row + 1] for row in range(4))
    rate = jnp.concatenate([rate, rate], axis=1)
    pre = dot(x, ws_ref[...].astype(BF16), LAST) + jnp.concatenate([bias_f, bias_b], axis=1)
    step = jnp.maximum(pre, 0.0) + jnp.log1p(jnp.exp(-jnp.abs(pre)))
    logs = -rate * step
    row, col = iota((SPAN, SPAN), 0), iota((SPAN, SPAN), 1)
    lower, upper = row > col, row < col
    exact = lax.Precision.HIGHEST
    ahead = dot((row >= col).astype(F32), logs, precision=exact)
    behind = dot((row <= col).astype(F32), logs, precision=exact)
    forward = iota(logs.shape, 1) < heads
    cum = jnp.where(forward, ahead, behind)
    total = jnp.where(forward[:1], cum[SPAN - 1 :], cum[:1])
    tail = jnp.exp(total - cum) * step
    reach_ref[...] = jnp.exp(cum)
    decay = jnp.exp(total)
    cum_t, step_t = cum.T, step.T

    ready(waits[0])
    maps = dot(x, wm_ref[...]).astype(BF16)
    in_f, out_f = maps[:, :STATE], maps[:, STATE : 2 * STATE]
    in_b, out_b = maps[:, 2 * STATE : 3 * STATE], maps[:, 3 * STATE :]
    out_ref[:, :STATE] = out_f
    out_ref[:, STATE:] = out_b
    scores = jnp.where(lower, dot(out_f, in_f, LAST), jnp.where(upper, dot(out_b, in_b, LAST), 0.0))
    in_f32, in_b32 = in_f.astype(F32), in_b.astype(F32)
    weights, tailed = [], []
    for h in range(heads):
        g = h + heads
        spread = jnp.where(
            lower,
            cum[:, h : h + 1] - cum_t[h : h + 1],
            cum[:, g : g + 1] - cum_t[g : g + 1],
        )
        steps = jnp.where(lower, step_t[h : h + 1], step_t[g : g + 1])
        weights.append((jnp.exp(spread) * (scores * steps)).astype(BF16))
        both = [in_f32 * tail[:, h : h + 1], in_b32 * tail[:, g : g + 1]]
        tailed.append(jnp.concatenate(both, axis=1).astype(BF16))
        marks = split(decay[:, h : h + 1], 0) + split(decay[:, g : g + 1], 2)
        send_ref[h, 2 * HEADDIM :] = marks.astype(BF16)

    ready(waits[1])
    inner = dot(x, wi_ref[...]).astype(BF16)
    left = iota((SPAN, 2 * HEADDIM), 1) < HEADDIM
    zero = jnp.zeros((SPAN, 2 * HEADDIM), BF16)
    for pair in range(heads // 2):
        here = slice(2 * HEADDIM * pair, 2 * HEADDIM * (pair + 1))
        both = inner[:, here]
        for h in (2 * pair, 2 * pair + 1):
            piece = dot(both[:, HEADDIM * (h % 2) : HEADDIM * (h % 2 + 1)], tailed[h], FIRST).astype(BF16)
            send_ref[h, :HEADDIM] = piece[:, :STATE]
            send_ref[h, HEADDIM : 2 * HEADDIM] = piece[:, STATE:]
        stacked = jnp.concatenate([jnp.where(left, both, zero), jnp.where(left, zero, both)], axis=0)
        gains = jnp.where(left, gain[:, 2 * pair : 2 * pair + 1], gain[:, 2 * pair + 1 : 2 * pair + 2])
        mixing = jnp.concatenate(weights[2 * pair : 2 * pair + 2], axis=1)
        y_ref[:, here] = dot(mixing, stacked) + gains * both.astype(F32)


def forward_part(rows):
    rows = rows.astype(F32)
    return joined(rows[2 * HEADDIM :], 0), rows[:HEADDIM]


def backward_part(rows):
    rows = rows.astype(F32)
    return joined(rows[2 * HEADDIM :], 2), rows[HEADDIM : 2 * HEADDIM]


def total_kernel(got_ref, send_ref):
    blocks, groups = got_ref.shape[0], send_ref.shape[0]
    place = lax.axis_index("zgroup")
    decay_f = decay_b = jnp.ones((1, STATE), F32)
    state_f = state_b = jnp.zeros((HEADDIM, STATE), F32)
    for block in range(blocks):
        decay, piece = forward_part(got_ref[block])
        decay_f, state_f = decay * decay_f, decay * state_f + piece
        decay, piece = backward_part(got_ref[blocks - 1 - block])
        decay_b, state_b = decay * decay_b, decay * state_b + piece
    marks_f, marks_b = split(decay_f, 0).astype(BF16), split(decay_b, 0).astype(BF16)
    state_f, state_b = state_f.astype(BF16), state_b.astype(BF16)
    for group in range(groups):
        later = group > place
        send_ref[group, :HEADDIM] = jnp.where(later, state_f, state_b)
        send_ref[group, HEADDIM:] = jnp.where(later, marks_f, marks_b)


def scan_kernel(totals_ref, got_ref, back_ref):
    blocks, groups = got_ref.shape[0], totals_ref.shape[0]
    place = lax.axis_index("zgroup")
    state_f = state_b = jnp.zeros((HEADDIM, STATE), F32)
    for group in range(groups):
        rows = totals_ref[group].astype(F32)
        state_f = jnp.where(group < place, joined(rows[HEADDIM:], 0) * state_f + rows[:HEADDIM], state_f)
        other = groups - 1 - group
        rows = totals_ref[other].astype(F32)
        state_b = jnp.where(other > place, joined(rows[HEADDIM:], 0) * state_b + rows[:HEADDIM], state_b)
    for block in range(blocks):
        back_ref[block, :HEADDIM] = state_f.astype(BF16)
        decay, piece = forward_part(got_ref[block])
        state_f = decay * state_f + piece
        other = blocks - 1 - block
        back_ref[other, HEADDIM:] = state_b.astype(BF16)
        decay, piece = backward_part(got_ref[other])
        state_b = decay * state_b + piece


def final_kernel(state_ref, out_ref, reach_ref, y_ref, mixed_ref):
    heads = state_ref.shape[0]
    ahead = state_ref[:, :HEADDIM].reshape(heads * HEADDIM, STATE)
    behind = state_ref[:, HEADDIM:].reshape(heads * HEADDIM, STATE)
    far_f = dot(out_ref[:, :STATE], ahead, LAST)
    far_b = dot(out_ref[:, STATE:], behind, LAST)
    reach = reach_ref[...]
    left = iota((SPAN, 2 * HEADDIM), 1) < HEADDIM
    for pair in range(heads // 2):
        here = slice(2 * HEADDIM * pair, 2 * HEADDIM * (pair + 1))
        h, g = 2 * pair, 2 * pair + heads
        scale_f = jnp.where(left, reach[:, h : h + 1], reach[:, h + 1 : h + 2])
        scale_b = jnp.where(left, reach[:, g : g + 1], reach[:, g + 1 : g + 2])
        mixed_ref[:, here] = (y_ref[:, here] + scale_f * far_f[:, here] + scale_b * far_b[:, here]).astype(BF16)


def call(kernel, out_shape, flops, **kwargs):
    return pl.pallas_call(
        kernel,
        out_shape=out_shape,
        compiler_params=pltpu.CompilerParams(vmem_limit_bytes=24 * 1024 * 1024),
        cost_estimate=pl.CostEstimate(flops=flops, bytes_accessed=1 << 20, transcendentals=0),
        **kwargs,
    )


def shards(hidden_in, w_inner, w_inout, w_step, step_bias, decay_rate, skip_gain):
    heads = w_step.shape[2]
    width = w_inner.shape[1]
    columns = lax.axis_size("y")
    groups = lax.axis_size("zgroup")
    shape = jax.ShapeDtypeStruct
    copies = jnp.broadcast_to(hidden_in[None], (columns, *hidden_in.shape))
    mine = lax.all_to_all(copies, "y", 0, 0, tiled=True)
    other = lax.ppermute(mine, "core", [(0, 1), (1, 0)])
    small = jnp.concatenate([step_bias, decay_rate[None], skip_gain[None]], axis=0)
    w_rows = w_step.transpose(0, 2, 1).reshape(2 * heads, -1).astype(F32)
    sources = (w_inout, w_inner)
    send, near, outs, reach = pl.pallas_call(
        local_kernel,
        out_shape=(
            shape((heads, 2 * HEADDIM + EXTRA, STATE), BF16),
            shape((SPAN, width), F32),
            shape((SPAN, 2 * STATE), BF16),
            shape((SPAN, 2 * heads), F32),
        ),
        in_specs=[VMEM] * 4 + [HBM] * len(sources),
        out_specs=(VMEM,) * 4,
        scratch_shapes=[pltpu.VMEM(a.shape, a.dtype) for a in sources]
        + [pltpu.SemaphoreType.DMA((CUTS * len(sources),))],
        compiler_params=pltpu.CompilerParams(vmem_limit_bytes=52 * 1024 * 1024),
        cost_estimate=pl.CostEstimate(flops=700_000_000, bytes_accessed=6 << 20, transcendentals=0),
    )(mine, other, w_rows, small, *sources)
    got = lax.all_to_all(send, ("zpair", "x"), 0, 0, tiled=True)
    totals = call(total_kernel, shape((groups, HEADDIM + EXTRA, STATE), BF16), 1_000_000)(got)
    totals = lax.all_to_all(totals, "zgroup", 0, 0, tiled=True)
    back = call(scan_kernel, shape((heads, 2 * HEADDIM, STATE), BF16), 1_000_000)(totals, got)
    state = lax.all_to_all(back, ("zpair", "x"), 0, 0, tiled=True)
    return call(final_kernel, shape((SPAN, width), BF16), 40_000_000)(state, outs, reach, near)


def solution(mesh):
    seq, head = mesh.shape["seq"], mesh.shape["head"]
    names = ("zgroup", "zpair", "x", "y", "core")
    fine = Mesh(mesh.devices.reshape(seq // 8, 2, 4, head // 2, 2), names)
    long, wide = ("zgroup", "zpair", "x"), ("y", "core")
    placed = (
        P((*long, *wide), None),
        P(None, wide),
        P(),
        P(None, None, wide),
        P(None, wide),
        P(wide),
        P(wide),
    )
    return jax.shard_map(
        shards, mesh=fine, in_specs=placed, out_specs=P(long, wide), check_vma=False
    )
```

```python
import jax
import jax.numpy as jnp
from jax import lax
from jax.experimental import pallas as pl
from jax.experimental.pallas import tpu as pltpu
from jax.sharding import Mesh, PartitionSpec as P

SPAN = 128
HEADDIM = 64
STATE = 128
EXTRA = 8
CUTS = 1
DEPTH = 2
F32 = jnp.float32
BF16 = jnp.bfloat16
LAST = (((1,), (1,)), ((), ()))
FIRST = (((0,), (0,)), ((), ()))
VMEM = pl.BlockSpec(memory_space=pltpu.VMEM)
HBM = pl.BlockSpec(memory_space=pltpu.HBM)


def dot(a, b, dims=None, precision=None):
    dims = dims or (((1,), (0,)), ((), ()))
    return lax.dot_general(a, b, dims, precision=precision, preferred_element_type=F32)


def iota(shape, dim):
    return lax.broadcasted_iota(jnp.int32, shape, dim)


def split(value, first):
    mark = iota((EXTRA, STATE), 0)
    high = value.astype(BF16).astype(F32)
    return jnp.where(mark == first, high, 0.0) + jnp.where(mark == first + 1, value - high, 0.0)


def joined(rows, first):
    return rows[first : first + 1] + rows[first + 1 : first + 2]


def fetch(pairs, sems):
    waits, used = [], 0
    for src, dst in pairs:
        cuts = CUTS if src.shape[0] % (16 * CUTS) == 0 else 1
        size = src.shape[0] // cuts
        copies = []
        for cut in range(cuts):
            part = pl.ds(cut * size, size)
            ends = (src.at[part], dst.at[part]) if cuts > 1 else (src, dst)
            copies.append(pltpu.make_async_copy(*ends, sems.at[used + cut]))
        used += cuts
        for copy in copies:
            copy.start()
        waits.append(copies)
    return waits


def ready(copies):
    for copy in copies:
        copy.wait()


def local_kernel(x_ref, *refs):
    sources, held, sems = refs[:6], refs[10:16], refs[16]
    send_ref, y_ref, out_ref, reach_ref = refs[6:10]
    ws_ref, bias_ref, rate_ref, gain_ref, wm_ref, wi_ref = held
    waits = fetch(zip(sources, held), sems)
    heads = ws_ref.shape[1]
    share = (send_ref.shape[1] - EXTRA) // 2
    parts = HEADDIM // share
    cores, columns = x_ref.shape[:2]
    x = jnp.concatenate([x_ref[core, y] for y in range(columns) for core in range(cores)], axis=0)
    for copies in waits[:4]:
        ready(copies)
    rate, gain = rate_ref[...].reshape(1, heads), gain_ref[...].reshape(1, heads)
    rate = jnp.concatenate([rate, rate], axis=1)
    pre = [dot(x, ws_ref[side], LAST) + bias_ref[side : side + 1] for side in range(2)]
    pre = jnp.concatenate(pre, axis=1)
    step = jnp.maximum(pre, 0.0) + jnp.log1p(jnp.exp(-jnp.abs(pre)))
    logs = -rate * step
    row, col = iota((SPAN, SPAN), 0), iota((SPAN, SPAN), 1)
    lower, upper = row > col, row < col
    exact = lax.Precision.HIGHEST
    ahead = dot((row >= col).astype(F32), logs, precision=exact)
    behind = dot((row <= col).astype(F32), logs, precision=exact)
    forward = iota(logs.shape, 1) < heads
    cum = jnp.where(forward, ahead, behind)
    total = jnp.where(forward[:1], cum[SPAN - 1 :], cum[:1])
    tail = jnp.exp(total - cum) * step
    reach_ref[...] = jnp.exp(cum)
    decay = jnp.exp(total)
    cum_t, step_t = cum.T, step.T

    ready(waits[4])
    maps = dot(x, wm_ref[...]).astype(BF16)
    in_f, out_f = maps[:, :STATE], maps[:, STATE : 2 * STATE]
    in_b, out_b = maps[:, 2 * STATE : 3 * STATE], maps[:, 3 * STATE :]
    out_ref[:, :STATE] = out_f
    out_ref[:, STATE:] = out_b
    scores = jnp.where(lower, dot(out_f, in_f, LAST), jnp.where(upper, dot(out_b, in_b, LAST), 0.0))
    in_f32, in_b32 = in_f.astype(F32), in_b.astype(F32)
    weights, tailed = [], []
    for h in range(heads):
        g = h + heads
        spread = jnp.where(
            lower,
            cum[:, h : h + 1] - cum_t[h : h + 1],
            cum[:, g : g + 1] - cum_t[g : g + 1],
        )
        steps = jnp.where(lower, step_t[h : h + 1], step_t[g : g + 1])
        weights.append((jnp.exp(spread) * (scores * steps)).astype(BF16))
        both = [in_f32 * tail[:, h : h + 1], in_b32 * tail[:, g : g + 1]]
        tailed.append(jnp.concatenate(both, axis=1).astype(BF16))
        marks = (split(decay[:, h : h + 1], 0) + split(decay[:, g : g + 1], 2)).astype(BF16)
        for part in range(h * parts, (h + 1) * parts):
            send_ref[part, 2 * share :] = marks

    ready(waits[5])
    inner = dot(x, wi_ref[...]).astype(BF16)
    left = iota((SPAN, 2 * HEADDIM), 1) < HEADDIM
    zero = jnp.zeros((SPAN, 2 * HEADDIM), BF16)
    for pair in range(heads // 2):
        here = slice(2 * HEADDIM * pair, 2 * HEADDIM * (pair + 1))
        both = inner[:, here]
        for h in (2 * pair, 2 * pair + 1):
            piece = dot(both[:, HEADDIM * (h % 2) : HEADDIM * (h % 2 + 1)], tailed[h], FIRST).astype(BF16)
            for part in range(parts):
                rows = slice(part * share, (part + 1) * share)
                send_ref[h * parts + part, :share] = piece[rows, :STATE]
                send_ref[h * parts + part, share : 2 * share] = piece[rows, STATE:]
        stacked = jnp.concatenate([jnp.where(left, both, zero), jnp.where(left, zero, both)], axis=0)
        gains = jnp.where(left, gain[:, 2 * pair : 2 * pair + 1], gain[:, 2 * pair + 1 : 2 * pair + 2])
        mixing = jnp.concatenate(weights[2 * pair : 2 * pair + 2], axis=1)
        y_ref[:, here] = dot(mixing, stacked) + gains * both.astype(F32)


def forward_part(rows, share):
    rows = rows.astype(F32)
    return joined(rows[2 * share :], 0), rows[:share]


def backward_part(rows, share):
    rows = rows.astype(F32)
    return joined(rows[2 * share :], 2), rows[share : 2 * share]


def total_kernel(got_ref, send_ref):
    blocks, share = got_ref.shape[0], (got_ref.shape[1] - EXTRA) // 2
    place = lax.axis_index("zgroup")
    decay_f = decay_b = jnp.ones((1, STATE), F32)
    state_f = state_b = jnp.zeros((share, STATE), F32)
    for block in range(blocks):
        decay, piece = forward_part(got_ref[block], share)
        decay_f, state_f = decay * decay_f, decay * state_f + piece
        decay, piece = backward_part(got_ref[blocks - 1 - block], share)
        decay_b, state_b = decay * decay_b, decay * state_b + piece
    marks_f, marks_b = split(decay_f, 0).astype(BF16), split(decay_b, 0).astype(BF16)
    state_f, state_b = state_f.astype(BF16), state_b.astype(BF16)
    for group in range(send_ref.shape[0]):
        later = group > place
        send_ref[group, :share] = jnp.where(later, state_f, state_b)
        send_ref[group, share:] = jnp.where(later, marks_f, marks_b)


def scan_kernel(totals_ref, got_ref, back_ref):
    blocks, share = got_ref.shape[0], back_ref.shape[1] // 2
    groups = totals_ref.shape[0]
    place = lax.axis_index("zgroup")
    state_f = state_b = jnp.zeros((share, STATE), F32)
    for group in range(groups):
        rows = totals_ref[group].astype(F32)
        state_f = jnp.where(group < place, joined(rows[share:], 0) * state_f + rows[:share], state_f)
        other = groups - 1 - group
        rows = totals_ref[other].astype(F32)
        state_b = jnp.where(other > place, joined(rows[share:], 0) * state_b + rows[:share], state_b)
    for block in range(blocks):
        back_ref[block, :share] = state_f.astype(BF16)
        decay, piece = forward_part(got_ref[block], share)
        state_f = decay * state_f + piece
        other = blocks - 1 - block
        back_ref[other, share:] = state_b.astype(BF16)
        decay, piece = backward_part(got_ref[other], share)
        state_b = decay * state_b + piece


def final_kernel(state_ref, out_ref, reach_ref, y_ref, mixed_ref):
    owners, rows, _ = state_ref.shape
    share, heads = rows // 2, reach_ref.shape[1] // 2
    ahead = state_ref[:, :share].reshape(owners * share, STATE)
    behind = state_ref[:, share:].reshape(owners * share, STATE)
    far_f = dot(out_ref[:, :STATE], ahead, LAST)
    far_b = dot(out_ref[:, STATE:], behind, LAST)
    reach = reach_ref[...]
    left = iota((SPAN, 2 * HEADDIM), 1) < HEADDIM
    for pair in range(heads // 2):
        here = slice(2 * HEADDIM * pair, 2 * HEADDIM * (pair + 1))
        h, g = 2 * pair, 2 * pair + heads
        scale_f = jnp.where(left, reach[:, h : h + 1], reach[:, h + 1 : h + 2])
        scale_b = jnp.where(left, reach[:, g : g + 1], reach[:, g + 1 : g + 2])
        mixed_ref[:, here] = (y_ref[:, here] + scale_f * far_f[:, here] + scale_b * far_b[:, here]).astype(BF16)


def call(kernel, out_shape, flops, **kwargs):
    return pl.pallas_call(
        kernel,
        out_shape=out_shape,
        compiler_params=pltpu.CompilerParams(vmem_limit_bytes=24 * 1024 * 1024),
        cost_estimate=pl.CostEstimate(flops=flops, bytes_accessed=1 << 20, transcendentals=0),
        **kwargs,
    )


def shards(hidden_in, w_inner, w_inout, w_step, step_bias, decay_rate, skip_gain):
    heads = w_step.shape[2]
    width = w_inner.shape[1]
    groups = lax.axis_size("zgroup")
    owners = lax.axis_size("zpart") * lax.axis_size("x")
    share = width // owners
    shape = jax.ShapeDtypeStruct
    copies = jnp.broadcast_to(hidden_in[None], (lax.axis_size("y"), *hidden_in.shape))
    x = lax.all_gather(lax.all_to_all(copies, "y", 0, 0, tiled=True), "core", axis=0)
    sources = (w_step.transpose(0, 2, 1), step_bias, decay_rate, skip_gain, w_inout, w_inner)
    sources = tuple(pltpu.with_memory_space_constraint(a, pltpu.HBM) for a in sources)
    send, near, outs, reach = pl.pallas_call(
        local_kernel,
        out_shape=(
            shape((owners, 2 * share + EXTRA, STATE), BF16),
            shape((SPAN, width), F32),
            shape((SPAN, 2 * STATE), BF16),
            shape((SPAN, 2 * heads), F32),
        ),
        in_specs=[VMEM] + [HBM] * len(sources),
        out_specs=(VMEM,) * 4,
        scratch_shapes=[pltpu.VMEM(a.shape, a.dtype) for a in sources]
        + [pltpu.SemaphoreType.DMA((CUTS * len(sources),))],
        compiler_params=pltpu.CompilerParams(vmem_limit_bytes=24 * 1024 * 1024),
        cost_estimate=pl.CostEstimate(flops=700_000_000, bytes_accessed=6 << 20, transcendentals=0),
    )(x, *sources)
    got = lax.all_to_all(send, ("zpart", "x"), 0, 0, tiled=True)
    totals = call(total_kernel, shape((groups, share + EXTRA, STATE), BF16), 1_000_000)(got)
    totals = lax.all_to_all(totals, "zgroup", 0, 0, tiled=True)
    back = call(scan_kernel, shape((owners, 2 * share, STATE), BF16), 1_000_000)(totals, got)
    state = lax.all_to_all(back, ("zpart", "x"), 0, 0, tiled=True)
    return call(final_kernel, shape((SPAN, width), BF16), 40_000_000)(state, outs, reach, near)


def solution(mesh):
    seq, head = mesh.shape["seq"], mesh.shape["head"]
    names = ("zgroup", "zpart", "x", "y", "core")
    fine = Mesh(mesh.devices.reshape(seq // (4 * DEPTH), DEPTH, 4, head // 2, 2), names)
    long, wide = ("zgroup", "zpart", "x"), ("y", "core")
    placed = (
        P((*long, *wide), None),
        P(None, wide),
        P(),
        P(None, None, wide),
        P(None, wide),
        P(wide),
        P(wide),
    )
    return jax.shard_map(
        shards, mesh=fine, in_specs=placed, out_specs=P(long, wide), check_vma=False
    )
```

```python
import jax
import jax.numpy as jnp
from jax import lax
from jax.experimental import pallas as pl
from jax.experimental.pallas import tpu as pltpu
from jax.sharding import Mesh, PartitionSpec as P

SPAN = 128
HEADDIM = 64
STATE = 128
EXTRA = 8
CUTS = 1
DEPTH = 2
Y_ORDER = (0, 2, 1, 3)
Z_ORDER = (0, 4, 2, 6, 1, 5, 3, 7)
F32 = jnp.float32
BF16 = jnp.bfloat16
LAST = (((1,), (1,)), ((), ()))
FIRST = (((0,), (0,)), ((), ()))
VMEM = pl.BlockSpec(memory_space=pltpu.VMEM)
HBM = pl.BlockSpec(memory_space=pltpu.HBM)


def dot(a, b, dims=None, precision=None):
    dims = dims or (((1,), (0,)), ((), ()))
    return lax.dot_general(a, b, dims, precision=precision, preferred_element_type=F32)


def iota(shape, dim):
    return lax.broadcasted_iota(jnp.int32, shape, dim)


def member(place, order):
    return jnp.where(lax.axis_index("core") == 0, order.index(place), len(order) - 1 - order.index(place))


def exchange(array, axis, order):
    groups = [[2 * place for place in order], [2 * place + 1 for place in reversed(order)]]
    return lax.all_to_all(array, (axis, "core"), 0, 0, tiled=True, axis_index_groups=groups)


def split(value, first):
    mark = iota((EXTRA, STATE), 0)
    high = value.astype(BF16).astype(F32)
    return jnp.where(mark == first, high, 0.0) + jnp.where(mark == first + 1, value - high, 0.0)


def joined(rows, first):
    return rows[first : first + 1] + rows[first + 1 : first + 2]


def fetch(pairs, sems):
    waits, used = [], 0
    for src, dst in pairs:
        cuts = CUTS if src.shape[0] % (16 * CUTS) == 0 else 1
        size = src.shape[0] // cuts
        copies = []
        for cut in range(cuts):
            part = pl.ds(cut * size, size)
            ends = (src.at[part], dst.at[part]) if cuts > 1 else (src, dst)
            copies.append(pltpu.make_async_copy(*ends, sems.at[used + cut]))
        used += cuts
        for copy in copies:
            copy.start()
        waits.append(copies)
    return waits


def ready(copies):
    for copy in copies:
        copy.wait()


def local_kernel(x_ref, *refs):
    sources, held, sems = refs[:6], refs[10:16], refs[16]
    send_ref, y_ref, out_ref, reach_ref = refs[6:10]
    ws_ref, bias_ref, rate_ref, gain_ref, wm_ref, wi_ref = held
    waits = fetch(zip(sources, held), sems)
    heads = ws_ref.shape[1]
    share = (send_ref.shape[1] - EXTRA) // 2
    parts = HEADDIM // share
    columns = x_ref.shape[1]
    places = [Y_ORDER.index(y) for y in range(columns)]
    x = [x_ref[core, columns - 1 - place if core else place] for place in places for core in range(2)]
    x = jnp.concatenate(x, axis=0)
    for copies in waits[:4]:
        ready(copies)
    rate, gain = rate_ref[...].reshape(1, heads), gain_ref[...].reshape(1, heads)
    rate = jnp.concatenate([rate, rate], axis=1)
    pre = [dot(x, ws_ref[side], LAST) + bias_ref[side : side + 1] for side in range(2)]
    pre = jnp.concatenate(pre, axis=1)
    step = jnp.maximum(pre, 0.0) + jnp.log1p(jnp.exp(-jnp.abs(pre)))
    logs = -rate * step
    row, col = iota((SPAN, SPAN), 0), iota((SPAN, SPAN), 1)
    lower, upper = row > col, row < col
    exact = lax.Precision.HIGHEST
    ahead = dot((row >= col).astype(F32), logs, precision=exact)
    behind = dot((row <= col).astype(F32), logs, precision=exact)
    forward = iota(logs.shape, 1) < heads
    cum = jnp.where(forward, ahead, behind)
    total = jnp.where(forward[:1], cum[SPAN - 1 :], cum[:1])
    tail = jnp.exp(total - cum) * step
    reach_ref[...] = jnp.exp(cum)
    decay = jnp.exp(total)
    cum_t, step_t = cum.T, step.T

    ready(waits[4])
    maps = dot(x, wm_ref[...]).astype(BF16)
    in_f, out_f = maps[:, :STATE], maps[:, STATE : 2 * STATE]
    in_b, out_b = maps[:, 2 * STATE : 3 * STATE], maps[:, 3 * STATE :]
    out_ref[:, :STATE] = out_f
    out_ref[:, STATE:] = out_b
    scores = jnp.where(lower, dot(out_f, in_f, LAST), jnp.where(upper, dot(out_b, in_b, LAST), 0.0))
    in_f32, in_b32 = in_f.astype(F32), in_b.astype(F32)
    weights, tailed = [], []
    for h in range(heads):
        g = h + heads
        spread = jnp.where(
            lower,
            cum[:, h : h + 1] - cum_t[h : h + 1],
            cum[:, g : g + 1] - cum_t[g : g + 1],
        )
        steps = jnp.where(lower, step_t[h : h + 1], step_t[g : g + 1])
        weights.append((jnp.exp(spread) * (scores * steps)).astype(BF16))
        both = [in_f32 * tail[:, h : h + 1], in_b32 * tail[:, g : g + 1]]
        tailed.append(jnp.concatenate(both, axis=1).astype(BF16))
        marks = (split(decay[:, h : h + 1], 0) + split(decay[:, g : g + 1], 2)).astype(BF16)
        for part in range(h * parts, (h + 1) * parts):
            send_ref[part, 2 * share :] = marks

    ready(waits[5])
    inner = dot(x, wi_ref[...]).astype(BF16)
    left = iota((SPAN, 2 * HEADDIM), 1) < HEADDIM
    zero = jnp.zeros((SPAN, 2 * HEADDIM), BF16)
    for pair in range(heads // 2):
        here = slice(2 * HEADDIM * pair, 2 * HEADDIM * (pair + 1))
        both = inner[:, here]
        for h in (2 * pair, 2 * pair + 1):
            piece = dot(both[:, HEADDIM * (h % 2) : HEADDIM * (h % 2 + 1)], tailed[h], FIRST).astype(BF16)
            for part in range(parts):
                rows = slice(part * share, (part + 1) * share)
                send_ref[h * parts + part, :share] = piece[rows, :STATE]
                send_ref[h * parts + part, share : 2 * share] = piece[rows, STATE:]
        stacked = jnp.concatenate([jnp.where(left, both, zero), jnp.where(left, zero, both)], axis=0)
        gains = jnp.where(left, gain[:, 2 * pair : 2 * pair + 1], gain[:, 2 * pair + 1 : 2 * pair + 2])
        mixing = jnp.concatenate(weights[2 * pair : 2 * pair + 2], axis=1)
        y_ref[:, here] = dot(mixing, stacked) + gains * both.astype(F32)


def forward_part(rows, share):
    rows = rows.astype(F32)
    return joined(rows[2 * share :], 0), rows[:share]


def backward_part(rows, share):
    rows = rows.astype(F32)
    return joined(rows[2 * share :], 2), rows[share : 2 * share]


def total_kernel(got_ref, send_ref):
    blocks, share = got_ref.shape[0], (got_ref.shape[1] - EXTRA) // 2
    place = lax.axis_index("zgroup")
    decay_f = decay_b = jnp.ones((1, STATE), F32)
    state_f = state_b = jnp.zeros((share, STATE), F32)
    for block in range(blocks):
        decay, piece = forward_part(got_ref[block], share)
        decay_f, state_f = decay * decay_f, decay * state_f + piece
        decay, piece = backward_part(got_ref[blocks - 1 - block], share)
        decay_b, state_b = decay * decay_b, decay * state_b + piece
    marks_f, marks_b = split(decay_f, 0).astype(BF16), split(decay_b, 0).astype(BF16)
    state_f, state_b = state_f.astype(BF16), state_b.astype(BF16)
    for group in range(send_ref.shape[0]):
        later, there = group > place, member(group, Z_ORDER)
        send_ref[there, :share] = jnp.where(later, state_f, state_b)
        send_ref[there, share:] = jnp.where(later, marks_f, marks_b)


def scan_kernel(totals_ref, got_ref, back_ref):
    blocks, share = got_ref.shape[0], back_ref.shape[1] // 2
    groups = totals_ref.shape[0]
    place = lax.axis_index("zgroup")
    state_f = state_b = jnp.zeros((share, STATE), F32)
    for group in range(groups):
        rows = totals_ref[member(group, Z_ORDER)].astype(F32)
        state_f = jnp.where(group < place, joined(rows[share:], 0) * state_f + rows[:share], state_f)
        other = groups - 1 - group
        rows = totals_ref[member(other, Z_ORDER)].astype(F32)
        state_b = jnp.where(other > place, joined(rows[share:], 0) * state_b + rows[:share], state_b)
    for block in range(blocks):
        back_ref[block, :share] = state_f.astype(BF16)
        decay, piece = forward_part(got_ref[block], share)
        state_f = decay * state_f + piece
        other = blocks - 1 - block
        back_ref[other, share:] = state_b.astype(BF16)
        decay, piece = backward_part(got_ref[other], share)
        state_b = decay * state_b + piece


def final_kernel(state_ref, out_ref, reach_ref, y_ref, mixed_ref):
    owners, rows, _ = state_ref.shape
    share, heads = rows // 2, reach_ref.shape[1] // 2
    ahead = state_ref[:, :share].reshape(owners * share, STATE)
    behind = state_ref[:, share:].reshape(owners * share, STATE)
    far_f = dot(out_ref[:, :STATE], ahead, LAST)
    far_b = dot(out_ref[:, STATE:], behind, LAST)
    reach = reach_ref[...]
    left = iota((SPAN, 2 * HEADDIM), 1) < HEADDIM
    for pair in range(heads // 2):
        here = slice(2 * HEADDIM * pair, 2 * HEADDIM * (pair + 1))
        h, g = 2 * pair, 2 * pair + heads
        scale_f = jnp.where(left, reach[:, h : h + 1], reach[:, h + 1 : h + 2])
        scale_b = jnp.where(left, reach[:, g : g + 1], reach[:, g + 1 : g + 2])
        mixed_ref[:, here] = (y_ref[:, here] + scale_f * far_f[:, here] + scale_b * far_b[:, here]).astype(BF16)


def call(kernel, out_shape, flops, **kwargs):
    return pl.pallas_call(
        kernel,
        out_shape=out_shape,
        compiler_params=pltpu.CompilerParams(vmem_limit_bytes=24 * 1024 * 1024),
        cost_estimate=pl.CostEstimate(flops=flops, bytes_accessed=1 << 20, transcendentals=0),
        **kwargs,
    )


def shards(hidden_in, w_inner, w_inout, w_step, step_bias, decay_rate, skip_gain):
    heads = w_step.shape[2]
    width = w_inner.shape[1]
    groups = lax.axis_size("zgroup")
    owners = lax.axis_size("zpart") * lax.axis_size("x")
    share = width // owners
    shape = jax.ShapeDtypeStruct
    copies = jnp.broadcast_to(hidden_in[None], (lax.axis_size("y"), *hidden_in.shape))
    x = lax.all_gather(exchange(copies, "y", Y_ORDER), "core", axis=0)
    sources = (w_step.transpose(0, 2, 1), step_bias, decay_rate, skip_gain, w_inout, w_inner)
    sources = tuple(pltpu.with_memory_space_constraint(a, pltpu.HBM) for a in sources)
    send, near, outs, reach = pl.pallas_call(
        local_kernel,
        out_shape=(
            shape((owners, 2 * share + EXTRA, STATE), BF16),
            shape((SPAN, width), F32),
            shape((SPAN, 2 * STATE), BF16),
            shape((SPAN, 2 * heads), F32),
        ),
        in_specs=[VMEM] + [HBM] * len(sources),
        out_specs=(VMEM,) * 4,
        scratch_shapes=[pltpu.VMEM(a.shape, a.dtype) for a in sources]
        + [pltpu.SemaphoreType.DMA((CUTS * len(sources),))],
        compiler_params=pltpu.CompilerParams(vmem_limit_bytes=24 * 1024 * 1024),
        cost_estimate=pl.CostEstimate(flops=700_000_000, bytes_accessed=6 << 20, transcendentals=0),
    )(x, *sources)
    got = lax.all_to_all(send, ("zpart", "x"), 0, 0, tiled=True)
    totals = call(total_kernel, shape((groups, share + EXTRA, STATE), BF16), 1_000_000)(got)
    totals = exchange(totals, "zgroup", Z_ORDER)
    back = call(scan_kernel, shape((owners, 2 * share, STATE), BF16), 1_000_000)(totals, got)
    state = lax.all_to_all(back, ("zpart", "x"), 0, 0, tiled=True)
    return call(final_kernel, shape((SPAN, width), BF16), 40_000_000)(state, outs, reach, near)


def solution(mesh):
    seq, head = mesh.shape["seq"], mesh.shape["head"]
    names = ("zgroup", "zpart", "x", "y", "core")
    fine = Mesh(mesh.devices.reshape(seq // (4 * DEPTH), DEPTH, 4, head // 2, 2), names)
    long, wide = ("zgroup", "zpart", "x"), ("y", "core")
    placed = (
        P((*long, *wide), None),
        P(None, wide),
        P(),
        P(None, None, wide),
        P(None, wide),
        P(wide),
        P(wide),
    )
    return jax.shard_map(
        shards, mesh=fine, in_specs=placed, out_specs=P(long, wide), check_vma=False
    )
```

```python
import jax
import jax.numpy as jnp
from jax import lax
from jax.experimental import pallas as pl
from jax.experimental.pallas import tpu as pltpu
from jax.sharding import Mesh, PartitionSpec as P

SPAN = 128
HEADDIM = 64
STATE = 128
EXTRA = 8
CUTS = 1
DEPTH = 2
Y_ORDER = (1, 3, 0, 2)
Z_ORDER = (3, 7, 1, 5, 2, 6, 0, 4)
F32 = jnp.float32
BF16 = jnp.bfloat16
LAST = (((1,), (1,)), ((), ()))
FIRST = (((0,), (0,)), ((), ()))
VMEM = pl.BlockSpec(memory_space=pltpu.VMEM)
HBM = pl.BlockSpec(memory_space=pltpu.HBM)


def dot(a, b, dims=None, precision=None):
    dims = dims or (((1,), (0,)), ((), ()))
    return lax.dot_general(a, b, dims, precision=precision, preferred_element_type=F32)


def iota(shape, dim):
    return lax.broadcasted_iota(jnp.int32, shape, dim)


def member(place, order):
    return jnp.where(lax.axis_index("core") == 0, order.index(place), len(order) - 1 - order.index(place))


def exchange(array, axis, order):
    groups = [[2 * place for place in order], [2 * place + 1 for place in reversed(order)]]
    return lax.all_to_all(array, (axis, "core"), 0, 0, tiled=True, axis_index_groups=groups)


def split(value, first):
    mark = iota((EXTRA, STATE), 0)
    high = value.astype(BF16).astype(F32)
    return jnp.where(mark == first, high, 0.0) + jnp.where(mark == first + 1, value - high, 0.0)


def joined(rows, first):
    return rows[first : first + 1] + rows[first + 1 : first + 2]


def fetch(pairs, sems):
    waits, used = [], 0
    for src, dst in pairs:
        cuts = CUTS if src.shape[0] % (16 * CUTS) == 0 else 1
        size = src.shape[0] // cuts
        copies = []
        for cut in range(cuts):
            part = pl.ds(cut * size, size)
            ends = (src.at[part], dst.at[part]) if cuts > 1 else (src, dst)
            copies.append(pltpu.make_async_copy(*ends, sems.at[used + cut]))
        used += cuts
        for copy in copies:
            copy.start()
        waits.append(copies)
    return waits


def ready(copies):
    for copy in copies:
        copy.wait()


def local_kernel(x_ref, *refs):
    sources, held, sems = refs[:6], refs[10:16], refs[16]
    send_ref, y_ref, out_ref, reach_ref = refs[6:10]
    ws_ref, bias_ref, rate_ref, gain_ref, wm_ref, wi_ref = held
    waits = fetch(zip(sources, held), sems)
    heads = ws_ref.shape[1]
    share = (send_ref.shape[1] - EXTRA) // 2
    parts = HEADDIM // share
    columns = x_ref.shape[1]
    places = [Y_ORDER.index(y) for y in range(columns)]
    x = [x_ref[core, columns - 1 - place if core else place] for place in places for core in range(2)]
    x = jnp.concatenate(x, axis=0)
    for copies in waits[:4]:
        ready(copies)
    rate, gain = rate_ref[...].reshape(1, heads), gain_ref[...].reshape(1, heads)
    rate = jnp.concatenate([rate, rate], axis=1)
    pre = [dot(x, ws_ref[side], LAST) + bias_ref[side : side + 1] for side in range(2)]
    pre = jnp.concatenate(pre, axis=1)
    step = jnp.maximum(pre, 0.0) + jnp.log1p(jnp.exp(-jnp.abs(pre)))
    logs = -rate * step
    row, col = iota((SPAN, SPAN), 0), iota((SPAN, SPAN), 1)
    lower, upper = row > col, row < col
    exact = lax.Precision.HIGHEST
    ahead = dot((row >= col).astype(F32), logs, precision=exact)
    behind = dot((row <= col).astype(F32), logs, precision=exact)
    forward = iota(logs.shape, 1) < heads
    cum = jnp.where(forward, ahead, behind)
    total = jnp.where(forward[:1], cum[SPAN - 1 :], cum[:1])
    tail = jnp.exp(total - cum) * step
    reach_ref[...] = jnp.exp(cum)
    decay = jnp.exp(total)
    cum_t, step_t = cum.T, step.T

    ready(waits[4])
    maps = dot(x, wm_ref[...]).astype(BF16)
    in_f, out_f = maps[:, :STATE], maps[:, STATE : 2 * STATE]
    in_b, out_b = maps[:, 2 * STATE : 3 * STATE], maps[:, 3 * STATE :]
    out_ref[:, :STATE] = out_f
    out_ref[:, STATE:] = out_b
    scores = jnp.where(lower, dot(out_f, in_f, LAST), jnp.where(upper, dot(out_b, in_b, LAST), 0.0))
    in_f32, in_b32 = in_f.astype(F32), in_b.astype(F32)
    weights, tailed = [], []
    for h in range(heads):
        g = h + heads
        spread = jnp.where(
            lower,
            cum[:, h : h + 1] - cum_t[h : h + 1],
            cum[:, g : g + 1] - cum_t[g : g + 1],
        )
        steps = jnp.where(lower, step_t[h : h + 1], step_t[g : g + 1])
        weights.append((jnp.exp(spread) * (scores * steps)).astype(BF16))
        both = [in_f32 * tail[:, h : h + 1], in_b32 * tail[:, g : g + 1]]
        tailed.append(jnp.concatenate(both, axis=1).astype(BF16))
        marks = (split(decay[:, h : h + 1], 0) + split(decay[:, g : g + 1], 2)).astype(BF16)
        for part in range(h * parts, (h + 1) * parts):
            send_ref[part, 2 * share :] = marks

    ready(waits[5])
    inner = dot(x, wi_ref[...]).astype(BF16)
    left = iota((SPAN, 2 * HEADDIM), 1) < HEADDIM
    zero = jnp.zeros((SPAN, 2 * HEADDIM), BF16)
    for pair in range(heads // 2):
        here = slice(2 * HEADDIM * pair, 2 * HEADDIM * (pair + 1))
        both = inner[:, here]
        for h in (2 * pair, 2 * pair + 1):
            piece = dot(both[:, HEADDIM * (h % 2) : HEADDIM * (h % 2 + 1)], tailed[h], FIRST).astype(BF16)
            for part in range(parts):
                rows = slice(part * share, (part + 1) * share)
                send_ref[h * parts + part, :share] = piece[rows, :STATE]
                send_ref[h * parts + part, share : 2 * share] = piece[rows, STATE:]
        stacked = jnp.concatenate([jnp.where(left, both, zero), jnp.where(left, zero, both)], axis=0)
        gains = jnp.where(left, gain[:, 2 * pair : 2 * pair + 1], gain[:, 2 * pair + 1 : 2 * pair + 2])
        mixing = jnp.concatenate(weights[2 * pair : 2 * pair + 2], axis=1)
        y_ref[:, here] = dot(mixing, stacked) + gains * both.astype(F32)


def forward_part(rows, share):
    rows = rows.astype(F32)
    return joined(rows[2 * share :], 0), rows[:share]


def backward_part(rows, share):
    rows = rows.astype(F32)
    return joined(rows[2 * share :], 2), rows[share : 2 * share]


def total_kernel(got_ref, send_ref):
    blocks, share = got_ref.shape[0], (got_ref.shape[1] - EXTRA) // 2
    place = lax.axis_index("zgroup")
    decay_f = decay_b = jnp.ones((1, STATE), F32)
    state_f = state_b = jnp.zeros((share, STATE), F32)
    for block in range(blocks):
        decay, piece = forward_part(got_ref[block], share)
        decay_f, state_f = decay * decay_f, decay * state_f + piece
        decay, piece = backward_part(got_ref[blocks - 1 - block], share)
        decay_b, state_b = decay * decay_b, decay * state_b + piece
    marks_f, marks_b = split(decay_f, 0).astype(BF16), split(decay_b, 0).astype(BF16)
    state_f, state_b = state_f.astype(BF16), state_b.astype(BF16)
    for group in range(send_ref.shape[0]):
        later, there = group > place, member(group, Z_ORDER)
        send_ref[there, :share] = jnp.where(later, state_f, state_b)
        send_ref[there, share:] = jnp.where(later, marks_f, marks_b)


def scan_kernel(totals_ref, got_ref, back_ref):
    blocks, share = got_ref.shape[0], back_ref.shape[1] // 2
    groups = totals_ref.shape[0]
    place = lax.axis_index("zgroup")
    state_f = state_b = jnp.zeros((share, STATE), F32)
    for group in range(groups):
        rows = totals_ref[member(group, Z_ORDER)].astype(F32)
        state_f = jnp.where(group < place, joined(rows[share:], 0) * state_f + rows[:share], state_f)
        other = groups - 1 - group
        rows = totals_ref[member(other, Z_ORDER)].astype(F32)
        state_b = jnp.where(other > place, joined(rows[share:], 0) * state_b + rows[:share], state_b)
    for block in range(blocks):
        back_ref[block, :share] = state_f.astype(BF16)
        decay, piece = forward_part(got_ref[block], share)
        state_f = decay * state_f + piece
        other = blocks - 1 - block
        back_ref[other, share:] = state_b.astype(BF16)
        decay, piece = backward_part(got_ref[other], share)
        state_b = decay * state_b + piece


def final_kernel(state_ref, out_ref, reach_ref, y_ref, mixed_ref):
    owners, rows, _ = state_ref.shape
    share, heads = rows // 2, reach_ref.shape[1] // 2
    ahead = state_ref[:, :share].reshape(owners * share, STATE)
    behind = state_ref[:, share:].reshape(owners * share, STATE)
    far_f = dot(out_ref[:, :STATE], ahead, LAST)
    far_b = dot(out_ref[:, STATE:], behind, LAST)
    reach = reach_ref[...]
    left = iota((SPAN, 2 * HEADDIM), 1) < HEADDIM
    for pair in range(heads // 2):
        here = slice(2 * HEADDIM * pair, 2 * HEADDIM * (pair + 1))
        h, g = 2 * pair, 2 * pair + heads
        scale_f = jnp.where(left, reach[:, h : h + 1], reach[:, h + 1 : h + 2])
        scale_b = jnp.where(left, reach[:, g : g + 1], reach[:, g + 1 : g + 2])
        mixed_ref[:, here] = (y_ref[:, here] + scale_f * far_f[:, here] + scale_b * far_b[:, here]).astype(BF16)


def call(kernel, out_shape, flops, **kwargs):
    return pl.pallas_call(
        kernel,
        out_shape=out_shape,
        compiler_params=pltpu.CompilerParams(vmem_limit_bytes=24 * 1024 * 1024),
        cost_estimate=pl.CostEstimate(flops=flops, bytes_accessed=1 << 20, transcendentals=0),
        **kwargs,
    )


def shards(hidden_in, w_inner, w_inout, w_step, step_bias, decay_rate, skip_gain):
    heads = w_step.shape[2]
    width = w_inner.shape[1]
    groups = lax.axis_size("zgroup")
    owners = lax.axis_size("zpart") * lax.axis_size("x")
    share = width // owners
    shape = jax.ShapeDtypeStruct
    copies = jnp.broadcast_to(hidden_in[None], (lax.axis_size("y"), *hidden_in.shape))
    x = lax.all_gather(exchange(copies, "y", Y_ORDER), "core", axis=0)
    sources = (w_step.transpose(0, 2, 1), step_bias, decay_rate, skip_gain, w_inout, w_inner)
    sources = tuple(pltpu.with_memory_space_constraint(a, pltpu.HBM) for a in sources)
    send, near, outs, reach = pl.pallas_call(
        local_kernel,
        out_shape=(
            shape((owners, 2 * share + EXTRA, STATE), BF16),
            shape((SPAN, width), F32),
            shape((SPAN, 2 * STATE), BF16),
            shape((SPAN, 2 * heads), F32),
        ),
        in_specs=[VMEM] + [HBM] * len(sources),
        out_specs=(VMEM,) * 4,
        scratch_shapes=[pltpu.VMEM(a.shape, a.dtype) for a in sources]
        + [pltpu.SemaphoreType.DMA((CUTS * len(sources),))],
        compiler_params=pltpu.CompilerParams(vmem_limit_bytes=24 * 1024 * 1024),
        cost_estimate=pl.CostEstimate(flops=700_000_000, bytes_accessed=6 << 20, transcendentals=0),
    )(x, *sources)
    got = lax.all_to_all(send, ("zpart", "x"), 0, 0, tiled=True)
    totals = call(total_kernel, shape((groups, share + EXTRA, STATE), BF16), 1_000_000)(got)
    totals = exchange(totals, "zgroup", Z_ORDER)
    back = call(scan_kernel, shape((owners, 2 * share, STATE), BF16), 1_000_000)(totals, got)
    state = lax.all_to_all(back, ("zpart", "x"), 0, 0, tiled=True)
    return call(final_kernel, shape((SPAN, width), BF16), 40_000_000)(state, outs, reach, near)


def solution(mesh):
    seq, head = mesh.shape["seq"], mesh.shape["head"]
    names = ("zgroup", "zpart", "x", "y", "core")
    fine = Mesh(mesh.devices.reshape(seq // (4 * DEPTH), DEPTH, 4, head // 2, 2), names)
    long, wide = ("zgroup", "zpart", "x"), ("y", "core")
    placed = (
        P((*long, *wide), None),
        P(None, wide),
        P(),
        P(None, None, wide),
        P(None, wide),
        P(wide),
        P(wide),
    )
    return jax.shard_map(
        shards, mesh=fine, in_specs=placed, out_specs=P(long, wide), check_vma=False
    )
```

```python
import jax
import jax.numpy as jnp
from jax import lax
from jax.experimental import pallas as pl
from jax.experimental.pallas import tpu as pltpu
from jax.sharding import Mesh, PartitionSpec as P

SPAN = 128
HEADDIM = 64
STATE = 128
EXTRA = 8
CUTS = 1
DEPTH = 2
L_ORDER = (2, 6, 1, 5, 3, 7, 0, 4)
Y_ORDER = (1, 3, 0, 2)
Z_ORDER = (3, 7, 1, 5, 2, 6, 0, 4)
F32 = jnp.float32
BF16 = jnp.bfloat16
LAST = (((1,), (1,)), ((), ()))
FIRST = (((0,), (0,)), ((), ()))
VMEM = pl.BlockSpec(memory_space=pltpu.VMEM)
HBM = pl.BlockSpec(memory_space=pltpu.HBM)


def dot(a, b, dims=None, precision=None):
    dims = dims or (((1,), (0,)), ((), ()))
    return lax.dot_general(a, b, dims, precision=precision, preferred_element_type=F32)


def iota(shape, dim):
    return lax.broadcasted_iota(jnp.int32, shape, dim)


def member(place, order):
    return jnp.where(lax.axis_index("core") == 0, order.index(place), len(order) - 1 - order.index(place))


def exchange(array, axes, order):
    groups = [[2 * place for place in order], [2 * place + 1 for place in reversed(order)]]
    return lax.all_to_all(array, (*axes, "core"), 0, 0, tiled=True, axis_index_groups=groups)


def split(value, first):
    mark = iota((EXTRA, STATE), 0)
    high = value.astype(BF16).astype(F32)
    return jnp.where(mark == first, high, 0.0) + jnp.where(mark == first + 1, value - high, 0.0)


def joined(rows, first):
    return rows[first : first + 1] + rows[first + 1 : first + 2]


def fetch(pairs, sems):
    waits, used = [], 0
    for src, dst in pairs:
        cuts = CUTS if src.shape[0] % (16 * CUTS) == 0 else 1
        size = src.shape[0] // cuts
        copies = []
        for cut in range(cuts):
            part = pl.ds(cut * size, size)
            ends = (src.at[part], dst.at[part]) if cuts > 1 else (src, dst)
            copies.append(pltpu.make_async_copy(*ends, sems.at[used + cut]))
        used += cuts
        for copy in copies:
            copy.start()
        waits.append(copies)
    return waits


def ready(copies):
    for copy in copies:
        copy.wait()


def local_kernel(x_ref, *refs):
    sources, held, sems = refs[:6], refs[10:16], refs[16]
    send_ref, y_ref, out_ref, reach_ref = refs[6:10]
    ws_ref, bias_ref, rate_ref, gain_ref, wm_ref, wi_ref = held
    waits = fetch(zip(sources, held), sems)
    heads = ws_ref.shape[1]
    share = (send_ref.shape[1] - EXTRA) // 2
    parts = HEADDIM // share
    columns = x_ref.shape[1]
    places = [Y_ORDER.index(y) for y in range(columns)]
    x = [x_ref[core, columns - 1 - place if core else place] for place in places for core in range(2)]
    x = jnp.concatenate(x, axis=0)
    for copies in waits[:4]:
        ready(copies)
    rate, gain = rate_ref[...].reshape(1, heads), gain_ref[...].reshape(1, heads)
    rate = jnp.concatenate([rate, rate], axis=1)
    pre = [dot(x, ws_ref[side], LAST) + bias_ref[side : side + 1] for side in range(2)]
    pre = jnp.concatenate(pre, axis=1)
    step = jnp.maximum(pre, 0.0) + jnp.log1p(jnp.exp(-jnp.abs(pre)))
    logs = -rate * step
    row, col = iota((SPAN, SPAN), 0), iota((SPAN, SPAN), 1)
    lower, upper = row > col, row < col
    exact = lax.Precision.HIGHEST
    ahead = dot((row >= col).astype(F32), logs, precision=exact)
    behind = dot((row <= col).astype(F32), logs, precision=exact)
    forward = iota(logs.shape, 1) < heads
    cum = jnp.where(forward, ahead, behind)
    total = jnp.where(forward[:1], cum[SPAN - 1 :], cum[:1])
    tail = jnp.exp(total - cum) * step
    reach_ref[...] = jnp.exp(cum)
    decay = jnp.exp(total)
    cum_t, step_t = cum.T, step.T

    ready(waits[4])
    maps = dot(x, wm_ref[...]).astype(BF16)
    in_f, out_f = maps[:, :STATE], maps[:, STATE : 2 * STATE]
    in_b, out_b = maps[:, 2 * STATE : 3 * STATE], maps[:, 3 * STATE :]
    out_ref[:, :STATE] = out_f
    out_ref[:, STATE:] = out_b
    scores = jnp.where(lower, dot(out_f, in_f, LAST), jnp.where(upper, dot(out_b, in_b, LAST), 0.0))
    in_f32, in_b32 = in_f.astype(F32), in_b.astype(F32)
    weights, tailed = [], []
    for h in range(heads):
        g = h + heads
        spread = jnp.where(
            lower,
            cum[:, h : h + 1] - cum_t[h : h + 1],
            cum[:, g : g + 1] - cum_t[g : g + 1],
        )
        steps = jnp.where(lower, step_t[h : h + 1], step_t[g : g + 1])
        weights.append((jnp.exp(spread) * (scores * steps)).astype(BF16))
        both = [in_f32 * tail[:, h : h + 1], in_b32 * tail[:, g : g + 1]]
        tailed.append(jnp.concatenate(both, axis=1).astype(BF16))
        marks = (split(decay[:, h : h + 1], 0) + split(decay[:, g : g + 1], 2)).astype(BF16)
        for part in range(h * parts, (h + 1) * parts):
            send_ref[member(part, L_ORDER), 2 * share :] = marks

    ready(waits[5])
    inner = dot(x, wi_ref[...]).astype(BF16)
    left = iota((SPAN, 2 * HEADDIM), 1) < HEADDIM
    zero = jnp.zeros((SPAN, 2 * HEADDIM), BF16)
    for pair in range(heads // 2):
        here = slice(2 * HEADDIM * pair, 2 * HEADDIM * (pair + 1))
        both = inner[:, here]
        for h in (2 * pair, 2 * pair + 1):
            piece = dot(both[:, HEADDIM * (h % 2) : HEADDIM * (h % 2 + 1)], tailed[h], FIRST).astype(BF16)
            for part in range(parts):
                rows = slice(part * share, (part + 1) * share)
                place = member(h * parts + part, L_ORDER)
                send_ref[place, :share] = piece[rows, :STATE]
                send_ref[place, share : 2 * share] = piece[rows, STATE:]
        stacked = jnp.concatenate([jnp.where(left, both, zero), jnp.where(left, zero, both)], axis=0)
        gains = jnp.where(left, gain[:, 2 * pair : 2 * pair + 1], gain[:, 2 * pair + 1 : 2 * pair + 2])
        mixing = jnp.concatenate(weights[2 * pair : 2 * pair + 2], axis=1)
        y_ref[:, here] = dot(mixing, stacked) + gains * both.astype(F32)


def forward_part(rows, share):
    rows = rows.astype(F32)
    return joined(rows[2 * share :], 0), rows[:share]


def backward_part(rows, share):
    rows = rows.astype(F32)
    return joined(rows[2 * share :], 2), rows[share : 2 * share]


def total_kernel(got_ref, send_ref):
    blocks, share = got_ref.shape[0], (got_ref.shape[1] - EXTRA) // 2
    place = lax.axis_index("zgroup")
    decay_f = decay_b = jnp.ones((1, STATE), F32)
    state_f = state_b = jnp.zeros((share, STATE), F32)
    for block in range(blocks):
        decay, piece = forward_part(got_ref[member(block, L_ORDER)], share)
        decay_f, state_f = decay * decay_f, decay * state_f + piece
        decay, piece = backward_part(got_ref[member(blocks - 1 - block, L_ORDER)], share)
        decay_b, state_b = decay * decay_b, decay * state_b + piece
    marks_f, marks_b = split(decay_f, 0).astype(BF16), split(decay_b, 0).astype(BF16)
    state_f, state_b = state_f.astype(BF16), state_b.astype(BF16)
    for group in range(send_ref.shape[0]):
        later, there = group > place, member(group, Z_ORDER)
        send_ref[there, :share] = jnp.where(later, state_f, state_b)
        send_ref[there, share:] = jnp.where(later, marks_f, marks_b)


def scan_kernel(totals_ref, got_ref, back_ref):
    blocks, share = got_ref.shape[0], back_ref.shape[1] // 2
    groups = totals_ref.shape[0]
    place = lax.axis_index("zgroup")
    state_f = state_b = jnp.zeros((share, STATE), F32)
    for group in range(groups):
        rows = totals_ref[member(group, Z_ORDER)].astype(F32)
        state_f = jnp.where(group < place, joined(rows[share:], 0) * state_f + rows[:share], state_f)
        other = groups - 1 - group
        rows = totals_ref[member(other, Z_ORDER)].astype(F32)
        state_b = jnp.where(other > place, joined(rows[share:], 0) * state_b + rows[:share], state_b)
    for block in range(blocks):
        here = member(block, L_ORDER)
        back_ref[here, :share] = state_f.astype(BF16)
        decay, piece = forward_part(got_ref[here], share)
        state_f = decay * state_f + piece
        other = member(blocks - 1 - block, L_ORDER)
        back_ref[other, share:] = state_b.astype(BF16)
        decay, piece = backward_part(got_ref[other], share)
        state_b = decay * state_b + piece


def final_kernel(state_ref, out_ref, reach_ref, y_ref, mixed_ref):
    owners, rows, _ = state_ref.shape
    share, heads = rows // 2, reach_ref.shape[1] // 2
    places = [member(owner, L_ORDER) for owner in range(owners)]
    ahead = jnp.concatenate([state_ref[place, :share] for place in places], axis=0)
    behind = jnp.concatenate([state_ref[place, share:] for place in places], axis=0)
    far_f = dot(out_ref[:, :STATE], ahead, LAST)
    far_b = dot(out_ref[:, STATE:], behind, LAST)
    reach = reach_ref[...]
    left = iota((SPAN, 2 * HEADDIM), 1) < HEADDIM
    for pair in range(heads // 2):
        here = slice(2 * HEADDIM * pair, 2 * HEADDIM * (pair + 1))
        h, g = 2 * pair, 2 * pair + heads
        scale_f = jnp.where(left, reach[:, h : h + 1], reach[:, h + 1 : h + 2])
        scale_b = jnp.where(left, reach[:, g : g + 1], reach[:, g + 1 : g + 2])
        mixed_ref[:, here] = (y_ref[:, here] + scale_f * far_f[:, here] + scale_b * far_b[:, here]).astype(BF16)


def call(kernel, out_shape, flops, **kwargs):
    return pl.pallas_call(
        kernel,
        out_shape=out_shape,
        compiler_params=pltpu.CompilerParams(vmem_limit_bytes=24 * 1024 * 1024),
        cost_estimate=pl.CostEstimate(flops=flops, bytes_accessed=1 << 20, transcendentals=0),
        **kwargs,
    )


def shards(hidden_in, w_inner, w_inout, w_step, step_bias, decay_rate, skip_gain):
    heads = w_step.shape[2]
    width = w_inner.shape[1]
    groups = lax.axis_size("zgroup")
    owners = lax.axis_size("zpart") * lax.axis_size("x")
    share = width // owners
    shape = jax.ShapeDtypeStruct
    copies = jnp.broadcast_to(hidden_in[None], (lax.axis_size("y"), *hidden_in.shape))
    x = lax.all_gather(exchange(copies, ("y",), Y_ORDER), "core", axis=0)
    sources = (w_step.transpose(0, 2, 1), step_bias, decay_rate, skip_gain, w_inout, w_inner)
    sources = tuple(pltpu.with_memory_space_constraint(a, pltpu.HBM) for a in sources)
    send, near, outs, reach = pl.pallas_call(
        local_kernel,
        out_shape=(
            shape((owners, 2 * share + EXTRA, STATE), BF16),
            shape((SPAN, width), F32),
            shape((SPAN, 2 * STATE), BF16),
            shape((SPAN, 2 * heads), F32),
        ),
        in_specs=[VMEM] + [HBM] * len(sources),
        out_specs=(VMEM,) * 4,
        scratch_shapes=[pltpu.VMEM(a.shape, a.dtype) for a in sources]
        + [pltpu.SemaphoreType.DMA((CUTS * len(sources),))],
        compiler_params=pltpu.CompilerParams(vmem_limit_bytes=24 * 1024 * 1024),
        cost_estimate=pl.CostEstimate(flops=700_000_000, bytes_accessed=6 << 20, transcendentals=0),
    )(x, *sources)
    got = exchange(send, ("zpart", "x"), L_ORDER)
    totals = call(total_kernel, shape((groups, share + EXTRA, STATE), BF16), 1_000_000)(got)
    totals = exchange(totals, ("zgroup",), Z_ORDER)
    back = call(scan_kernel, shape((owners, 2 * share, STATE), BF16), 1_000_000)(totals, got)
    state = exchange(back, ("zpart", "x"), L_ORDER)
    return call(final_kernel, shape((SPAN, width), BF16), 40_000_000)(state, outs, reach, near)


def solution(mesh):
    seq, head = mesh.shape["seq"], mesh.shape["head"]
    names = ("zgroup", "zpart", "x", "y", "core")
    fine = Mesh(mesh.devices.reshape(seq // (4 * DEPTH), DEPTH, 4, head // 2, 2), names)
    long, wide = ("zgroup", "zpart", "x"), ("y", "core")
    placed = (
        P((*long, *wide), None),
        P(None, wide),
        P(),
        P(None, None, wide),
        P(None, wide),
        P(wide),
        P(wide),
    )
    return jax.shard_map(
        shards, mesh=fine, in_specs=placed, out_specs=P(long, wide), check_vma=False
    )
```

```python
import jax
import jax.numpy as jnp
from jax import lax
from jax.experimental import pallas as pl
from jax.experimental.pallas import tpu as pltpu
from jax.sharding import Mesh, PartitionSpec as P

SPAN = 128
HEADDIM = 64
STATE = 128
EXTRA = 8
CUTS = 1
DEPTH = 2
L_ORDER = (2, 6, 3, 7, 1, 5, 0, 4)
Y_ORDER = (2, 0, 3, 1)
Z_ORDER = (3, 7, 1, 5, 2, 6, 0, 4)
F32 = jnp.float32
BF16 = jnp.bfloat16
LAST = (((1,), (1,)), ((), ()))
FIRST = (((0,), (0,)), ((), ()))
VMEM = pl.BlockSpec(memory_space=pltpu.VMEM)
HBM = pl.BlockSpec(memory_space=pltpu.HBM)


def dot(a, b, dims=None, precision=None):
    dims = dims or (((1,), (0,)), ((), ()))
    return lax.dot_general(a, b, dims, precision=precision, preferred_element_type=F32)


def iota(shape, dim):
    return lax.broadcasted_iota(jnp.int32, shape, dim)


def member(place, order):
    return jnp.where(lax.axis_index("core") == 0, order.index(place), len(order) - 1 - order.index(place))


def exchange(array, axes, order):
    groups = [[2 * place for place in order], [2 * place + 1 for place in reversed(order)]]
    return lax.all_to_all(array, (*axes, "core"), 0, 0, tiled=True, axis_index_groups=groups)


def split(value, first):
    mark = iota((EXTRA, STATE), 0)
    high = value.astype(BF16).astype(F32)
    return jnp.where(mark == first, high, 0.0) + jnp.where(mark == first + 1, value - high, 0.0)


def joined(rows, first):
    return rows[first : first + 1] + rows[first + 1 : first + 2]


def fetch(pairs, sems):
    waits, used = [], 0
    for src, dst in pairs:
        cuts = CUTS if src.shape[0] % (16 * CUTS) == 0 else 1
        size = src.shape[0] // cuts
        copies = []
        for cut in range(cuts):
            part = pl.ds(cut * size, size)
            ends = (src.at[part], dst.at[part]) if cuts > 1 else (src, dst)
            copies.append(pltpu.make_async_copy(*ends, sems.at[used + cut]))
        used += cuts
        for copy in copies:
            copy.start()
        waits.append(copies)
    return waits


def ready(copies):
    for copy in copies:
        copy.wait()


def local_kernel(x_ref, *refs):
    sources, held, sems = refs[:6], refs[10:16], refs[16]
    send_ref, y_ref, out_ref, reach_ref = refs[6:10]
    ws_ref, bias_ref, rate_ref, gain_ref, wm_ref, wi_ref = held
    waits = fetch(zip(sources, held), sems)
    heads = ws_ref.shape[1]
    share = (send_ref.shape[1] - EXTRA) // 2
    parts = HEADDIM // share
    columns = x_ref.shape[1]
    places = [Y_ORDER.index(y) for y in range(columns)]
    x = [x_ref[core, columns - 1 - place if core else place] for place in places for core in range(2)]
    x = jnp.concatenate(x, axis=0)
    for copies in waits[:4]:
        ready(copies)
    rate, gain = rate_ref[...].reshape(1, heads), gain_ref[...].reshape(1, heads)
    rate = jnp.concatenate([rate, rate], axis=1)
    pre = [dot(x, ws_ref[side], LAST) + bias_ref[side : side + 1] for side in range(2)]
    pre = jnp.concatenate(pre, axis=1)
    step = jnp.maximum(pre, 0.0) + jnp.log1p(jnp.exp(-jnp.abs(pre)))
    logs = -rate * step
    row, col = iota((SPAN, SPAN), 0), iota((SPAN, SPAN), 1)
    lower, upper = row > col, row < col
    exact = lax.Precision.HIGHEST
    ahead = dot((row >= col).astype(F32), logs, precision=exact)
    behind = dot((row <= col).astype(F32), logs, precision=exact)
    forward = iota(logs.shape, 1) < heads
    cum = jnp.where(forward, ahead, behind)
    total = jnp.where(forward[:1], cum[SPAN - 1 :], cum[:1])
    tail = jnp.exp(total - cum) * step
    reach_ref[...] = jnp.exp(cum)
    decay = jnp.exp(total)
    cum_t, step_t = cum.T, step.T

    ready(waits[4])
    maps = dot(x, wm_ref[...]).astype(BF16)
    in_f, out_f = maps[:, :STATE], maps[:, STATE : 2 * STATE]
    in_b, out_b = maps[:, 2 * STATE : 3 * STATE], maps[:, 3 * STATE :]
    out_ref[:, :STATE] = out_f
    out_ref[:, STATE:] = out_b
    scores = jnp.where(lower, dot(out_f, in_f, LAST), jnp.where(upper, dot(out_b, in_b, LAST), 0.0))
    in_f32, in_b32 = in_f.astype(F32), in_b.astype(F32)
    weights, tailed = [], []
    for h in range(heads):
        g = h + heads
        spread = jnp.where(
            lower,
            cum[:, h : h + 1] - cum_t[h : h + 1],
            cum[:, g : g + 1] - cum_t[g : g + 1],
        )
        steps = jnp.where(lower, step_t[h : h + 1], step_t[g : g + 1])
        weights.append((jnp.exp(spread) * (scores * steps)).astype(BF16))
        both = [in_f32 * tail[:, h : h + 1], in_b32 * tail[:, g : g + 1]]
        tailed.append(jnp.concatenate(both, axis=1).astype(BF16))
        marks = (split(decay[:, h : h + 1], 0) + split(decay[:, g : g + 1], 2)).astype(BF16)
        for part in range(h * parts, (h + 1) * parts):
            send_ref[member(part, L_ORDER), 2 * share :] = marks

    ready(waits[5])
    inner = dot(x, wi_ref[...]).astype(BF16)
    left = iota((SPAN, 2 * HEADDIM), 1) < HEADDIM
    zero = jnp.zeros((SPAN, 2 * HEADDIM), BF16)
    for pair in range(heads // 2):
        here = slice(2 * HEADDIM * pair, 2 * HEADDIM * (pair + 1))
        both = inner[:, here]
        for h in (2 * pair, 2 * pair + 1):
            piece = dot(both[:, HEADDIM * (h % 2) : HEADDIM * (h % 2 + 1)], tailed[h], FIRST).astype(BF16)
            for part in range(parts):
                rows = slice(part * share, (part + 1) * share)
                place = member(h * parts + part, L_ORDER)
                send_ref[place, :share] = piece[rows, :STATE]
                send_ref[place, share : 2 * share] = piece[rows, STATE:]
        stacked = jnp.concatenate([jnp.where(left, both, zero), jnp.where(left, zero, both)], axis=0)
        gains = jnp.where(left, gain[:, 2 * pair : 2 * pair + 1], gain[:, 2 * pair + 1 : 2 * pair + 2])
        mixing = jnp.concatenate(weights[2 * pair : 2 * pair + 2], axis=1)
        y_ref[:, here] = dot(mixing, stacked) + gains * both.astype(F32)


def forward_part(rows, share):
    rows = rows.astype(F32)
    return joined(rows[2 * share :], 0), rows[:share]


def backward_part(rows, share):
    rows = rows.astype(F32)
    return joined(rows[2 * share :], 2), rows[share : 2 * share]


def total_kernel(got_ref, send_ref):
    blocks, share = got_ref.shape[0], (got_ref.shape[1] - EXTRA) // 2
    place = lax.axis_index("zgroup")
    decay_f = decay_b = jnp.ones((1, STATE), F32)
    state_f = state_b = jnp.zeros((share, STATE), F32)
    for block in range(blocks):
        decay, piece = forward_part(got_ref[member(block, L_ORDER)], share)
        decay_f, state_f = decay * decay_f, decay * state_f + piece
        decay, piece = backward_part(got_ref[member(blocks - 1 - block, L_ORDER)], share)
        decay_b, state_b = decay * decay_b, decay * state_b + piece
    marks_f, marks_b = split(decay_f, 0).astype(BF16), split(decay_b, 0).astype(BF16)
    state_f, state_b = state_f.astype(BF16), state_b.astype(BF16)
    for group in range(send_ref.shape[0]):
        later, there = group > place, member(group, Z_ORDER)
        send_ref[there, :share] = jnp.where(later, state_f, state_b)
        send_ref[there, share:] = jnp.where(later, marks_f, marks_b)


def scan_kernel(totals_ref, got_ref, back_ref):
    blocks, share = got_ref.shape[0], back_ref.shape[1] // 2
    groups = totals_ref.shape[0]
    place = lax.axis_index("zgroup")
    state_f = state_b = jnp.zeros((share, STATE), F32)
    for group in range(groups):
        rows = totals_ref[member(group, Z_ORDER)].astype(F32)
        state_f = jnp.where(group < place, joined(rows[share:], 0) * state_f + rows[:share], state_f)
        other = groups - 1 - group
        rows = totals_ref[member(other, Z_ORDER)].astype(F32)
        state_b = jnp.where(other > place, joined(rows[share:], 0) * state_b + rows[:share], state_b)
    for block in range(blocks):
        here = member(block, L_ORDER)
        back_ref[here, :share] = state_f.astype(BF16)
        decay, piece = forward_part(got_ref[here], share)
        state_f = decay * state_f + piece
        other = member(blocks - 1 - block, L_ORDER)
        back_ref[other, share:] = state_b.astype(BF16)
        decay, piece = backward_part(got_ref[other], share)
        state_b = decay * state_b + piece


def final_kernel(state_ref, out_ref, reach_ref, y_ref, mixed_ref):
    owners, rows, _ = state_ref.shape
    share, heads = rows // 2, reach_ref.shape[1] // 2
    places = [member(owner, L_ORDER) for owner in range(owners)]
    ahead = jnp.concatenate([state_ref[place, :share] for place in places], axis=0)
    behind = jnp.concatenate([state_ref[place, share:] for place in places], axis=0)
    far_f = dot(out_ref[:, :STATE], ahead, LAST)
    far_b = dot(out_ref[:, STATE:], behind, LAST)
    reach = reach_ref[...]
    left = iota((SPAN, 2 * HEADDIM), 1) < HEADDIM
    for pair in range(heads // 2):
        here = slice(2 * HEADDIM * pair, 2 * HEADDIM * (pair + 1))
        h, g = 2 * pair, 2 * pair + heads
        scale_f = jnp.where(left, reach[:, h : h + 1], reach[:, h + 1 : h + 2])
        scale_b = jnp.where(left, reach[:, g : g + 1], reach[:, g + 1 : g + 2])
        mixed_ref[:, here] = (y_ref[:, here] + scale_f * far_f[:, here] + scale_b * far_b[:, here]).astype(BF16)


def call(kernel, out_shape, flops, **kwargs):
    return pl.pallas_call(
        kernel,
        out_shape=out_shape,
        compiler_params=pltpu.CompilerParams(vmem_limit_bytes=24 * 1024 * 1024),
        cost_estimate=pl.CostEstimate(flops=flops, bytes_accessed=1 << 20, transcendentals=0),
        **kwargs,
    )


def shards(hidden_in, w_inner, w_inout, w_step, step_bias, decay_rate, skip_gain):
    heads = w_step.shape[2]
    width = w_inner.shape[1]
    groups = lax.axis_size("zgroup")
    owners = lax.axis_size("zpart") * lax.axis_size("x")
    share = width // owners
    shape = jax.ShapeDtypeStruct
    copies = jnp.broadcast_to(hidden_in[None], (lax.axis_size("y"), *hidden_in.shape))
    x = lax.all_gather(exchange(copies, ("y",), Y_ORDER), "core", axis=0)
    sources = (w_step.transpose(0, 2, 1), step_bias, decay_rate, skip_gain, w_inout, w_inner)
    sources = tuple(pltpu.with_memory_space_constraint(a, pltpu.HBM) for a in sources)
    send, near, outs, reach = pl.pallas_call(
        local_kernel,
        out_shape=(
            shape((owners, 2 * share + EXTRA, STATE), BF16),
            shape((SPAN, width), F32),
            shape((SPAN, 2 * STATE), BF16),
            shape((SPAN, 2 * heads), F32),
        ),
        in_specs=[VMEM] + [HBM] * len(sources),
        out_specs=(VMEM,) * 4,
        scratch_shapes=[pltpu.VMEM(a.shape, a.dtype) for a in sources]
        + [pltpu.SemaphoreType.DMA((CUTS * len(sources),))],
        compiler_params=pltpu.CompilerParams(vmem_limit_bytes=24 * 1024 * 1024),
        cost_estimate=pl.CostEstimate(flops=700_000_000, bytes_accessed=6 << 20, transcendentals=0),
    )(x, *sources)
    got = exchange(send, ("zpart", "x"), L_ORDER)
    totals = call(total_kernel, shape((groups, share + EXTRA, STATE), BF16), 1_000_000)(got)
    totals = exchange(totals, ("zgroup",), Z_ORDER)
    back = call(scan_kernel, shape((owners, 2 * share, STATE), BF16), 1_000_000)(totals, got)
    state = exchange(back, ("zpart", "x"), L_ORDER)
    return call(final_kernel, shape((SPAN, width), BF16), 40_000_000)(state, outs, reach, near)


def solution(mesh):
    seq, head = mesh.shape["seq"], mesh.shape["head"]
    names = ("zgroup", "zpart", "x", "y", "core")
    fine = Mesh(mesh.devices.reshape(seq // (4 * DEPTH), DEPTH, 4, head // 2, 2), names)
    long, wide = ("zgroup", "zpart", "x"), ("y", "core")
    placed = (
        P((*long, *wide), None),
        P(None, wide),
        P(),
        P(None, None, wide),
        P(None, wide),
        P(wide),
        P(wide),
    )
    return jax.shard_map(
        shards, mesh=fine, in_specs=placed, out_specs=P(long, wide), check_vma=False
    )
```

```python
import jax
import jax.numpy as jnp
from jax import lax
from jax.experimental import pallas as pl
from jax.experimental.pallas import tpu as pltpu
from jax.sharding import Mesh, PartitionSpec as P

SPAN = 128
HEADDIM = 64
STATE = 128
EXTRA = 8
CUTS = 1
DEPTH = 2
L_ORDER = (2, 6, 3, 7, 1, 5, 0, 4)
Y_ORDER = (1, 2, 0, 3)
Z_ORDER = (3, 7, 1, 5, 2, 6, 0, 4)
F32 = jnp.float32
BF16 = jnp.bfloat16
LAST = (((1,), (1,)), ((), ()))
FIRST = (((0,), (0,)), ((), ()))
VMEM = pl.BlockSpec(memory_space=pltpu.VMEM)
HBM = pl.BlockSpec(memory_space=pltpu.HBM)


def dot(a, b, dims=None, precision=None):
    dims = dims or (((1,), (0,)), ((), ()))
    return lax.dot_general(a, b, dims, precision=precision, preferred_element_type=F32)


def iota(shape, dim):
    return lax.broadcasted_iota(jnp.int32, shape, dim)


def member(place, order):
    return jnp.where(lax.axis_index("core") == 0, order.index(place), len(order) - 1 - order.index(place))


def exchange(array, axes, order):
    groups = [[2 * place for place in order], [2 * place + 1 for place in reversed(order)]]
    return lax.all_to_all(array, (*axes, "core"), 0, 0, tiled=True, axis_index_groups=groups)


def split(value, first):
    mark = iota((EXTRA, STATE), 0)
    high = value.astype(BF16).astype(F32)
    return jnp.where(mark == first, high, 0.0) + jnp.where(mark == first + 1, value - high, 0.0)


def joined(rows, first):
    return rows[first : first + 1] + rows[first + 1 : first + 2]


def fetch(pairs, sems):
    waits, used = [], 0
    for src, dst in pairs:
        cuts = CUTS if src.shape[0] % (16 * CUTS) == 0 else 1
        size = src.shape[0] // cuts
        copies = []
        for cut in range(cuts):
            part = pl.ds(cut * size, size)
            ends = (src.at[part], dst.at[part]) if cuts > 1 else (src, dst)
            copies.append(pltpu.make_async_copy(*ends, sems.at[used + cut]))
        used += cuts
        for copy in copies:
            copy.start()
        waits.append(copies)
    return waits


def ready(copies):
    for copy in copies:
        copy.wait()


def local_kernel(x_ref, *refs):
    sources, held, sems = refs[:6], refs[10:16], refs[16]
    send_ref, y_ref, out_ref, reach_ref = refs[6:10]
    ws_ref, bias_ref, rate_ref, gain_ref, wm_ref, wi_ref = held
    waits = fetch(zip(sources, held), sems)
    heads = ws_ref.shape[1]
    share = (send_ref.shape[1] - EXTRA) // 2
    parts = HEADDIM // share
    columns = x_ref.shape[1]
    places = [Y_ORDER.index(y) for y in range(columns)]
    x = [x_ref[core, columns - 1 - place if core else place] for place in places for core in range(2)]
    x = jnp.concatenate(x, axis=0)
    for copies in waits[:4]:
        ready(copies)
    rate, gain = rate_ref[...].reshape(1, heads), gain_ref[...].reshape(1, heads)
    rate = jnp.concatenate([rate, rate], axis=1)
    pre = [dot(x, ws_ref[side], LAST) + bias_ref[side : side + 1] for side in range(2)]
    pre = jnp.concatenate(pre, axis=1)
    step = jnp.maximum(pre, 0.0) + jnp.log1p(jnp.exp(-jnp.abs(pre)))
    logs = -rate * step
    row, col = iota((SPAN, SPAN), 0), iota((SPAN, SPAN), 1)
    lower, upper = row > col, row < col
    exact = lax.Precision.HIGHEST
    ahead = dot((row >= col).astype(F32), logs, precision=exact)
    behind = dot((row <= col).astype(F32), logs, precision=exact)
    forward = iota(logs.shape, 1) < heads
    cum = jnp.where(forward, ahead, behind)
    total = jnp.where(forward[:1], cum[SPAN - 1 :], cum[:1])
    tail = jnp.exp(total - cum) * step
    reach_ref[...] = jnp.exp(cum)
    decay = jnp.exp(total)
    cum_t, step_t = cum.T, step.T

    ready(waits[4])
    maps = dot(x, wm_ref[...]).astype(BF16)
    in_f, out_f = maps[:, :STATE], maps[:, STATE : 2 * STATE]
    in_b, out_b = maps[:, 2 * STATE : 3 * STATE], maps[:, 3 * STATE :]
    out_ref[:, :STATE] = out_f
    out_ref[:, STATE:] = out_b
    scores = jnp.where(lower, dot(out_f, in_f, LAST), jnp.where(upper, dot(out_b, in_b, LAST), 0.0))
    in_f32, in_b32 = in_f.astype(F32), in_b.astype(F32)
    weights, tailed = [], []
    for h in range(heads):
        g = h + heads
        spread = jnp.where(
            lower,
            cum[:, h : h + 1] - cum_t[h : h + 1],
            cum[:, g : g + 1] - cum_t[g : g + 1],
        )
        steps = jnp.where(lower, step_t[h : h + 1], step_t[g : g + 1])
        weights.append((jnp.exp(spread) * (scores * steps)).astype(BF16))
        both = [in_f32 * tail[:, h : h + 1], in_b32 * tail[:, g : g + 1]]
        tailed.append(jnp.concatenate(both, axis=1).astype(BF16))
        marks = (split(decay[:, h : h + 1], 0) + split(decay[:, g : g + 1], 2)).astype(BF16)
        for part in range(h * parts, (h + 1) * parts):
            send_ref[member(part, L_ORDER), 2 * share :] = marks

    ready(waits[5])
    inner = dot(x, wi_ref[...]).astype(BF16)
    left = iota((SPAN, 2 * HEADDIM), 1) < HEADDIM
    zero = jnp.zeros((SPAN, 2 * HEADDIM), BF16)
    for pair in range(heads // 2):
        here = slice(2 * HEADDIM * pair, 2 * HEADDIM * (pair + 1))
        both = inner[:, here]
        for h in (2 * pair, 2 * pair + 1):
            piece = dot(both[:, HEADDIM * (h % 2) : HEADDIM * (h % 2 + 1)], tailed[h], FIRST).astype(BF16)
            for part in range(parts):
                rows = slice(part * share, (part + 1) * share)
                place = member(h * parts + part, L_ORDER)
                send_ref[place, :share] = piece[rows, :STATE]
                send_ref[place, share : 2 * share] = piece[rows, STATE:]
        stacked = jnp.concatenate([jnp.where(left, both, zero), jnp.where(left, zero, both)], axis=0)
        gains = jnp.where(left, gain[:, 2 * pair : 2 * pair + 1], gain[:, 2 * pair + 1 : 2 * pair + 2])
        mixing = jnp.concatenate(weights[2 * pair : 2 * pair + 2], axis=1)
        y_ref[:, here] = dot(mixing, stacked) + gains * both.astype(F32)


def forward_part(rows, share):
    rows = rows.astype(F32)
    return joined(rows[2 * share :], 0), rows[:share]


def backward_part(rows, share):
    rows = rows.astype(F32)
    return joined(rows[2 * share :], 2), rows[share : 2 * share]


def total_kernel(got_ref, send_ref):
    blocks, share = got_ref.shape[0], (got_ref.shape[1] - EXTRA) // 2
    place = lax.axis_index("zgroup")
    decay_f = decay_b = jnp.ones((1, STATE), F32)
    state_f = state_b = jnp.zeros((share, STATE), F32)
    for block in range(blocks):
        decay, piece = forward_part(got_ref[member(block, L_ORDER)], share)
        decay_f, state_f = decay * decay_f, decay * state_f + piece
        decay, piece = backward_part(got_ref[member(blocks - 1 - block, L_ORDER)], share)
        decay_b, state_b = decay * decay_b, decay * state_b + piece
    marks_f, marks_b = split(decay_f, 0).astype(BF16), split(decay_b, 0).astype(BF16)
    state_f, state_b = state_f.astype(BF16), state_b.astype(BF16)
    for group in range(send_ref.shape[0]):
        later, there = group > place, member(group, Z_ORDER)
        send_ref[there, :share] = jnp.where(later, state_f, state_b)
        send_ref[there, share:] = jnp.where(later, marks_f, marks_b)


def scan_kernel(totals_ref, got_ref, back_ref):
    blocks, share = got_ref.shape[0], back_ref.shape[1] // 2
    groups = totals_ref.shape[0]
    place = lax.axis_index("zgroup")
    state_f = state_b = jnp.zeros((share, STATE), F32)
    for group in range(groups):
        rows = totals_ref[member(group, Z_ORDER)].astype(F32)
        state_f = jnp.where(group < place, joined(rows[share:], 0) * state_f + rows[:share], state_f)
        other = groups - 1 - group
        rows = totals_ref[member(other, Z_ORDER)].astype(F32)
        state_b = jnp.where(other > place, joined(rows[share:], 0) * state_b + rows[:share], state_b)
    for block in range(blocks):
        here = member(block, L_ORDER)
        back_ref[here, :share] = state_f.astype(BF16)
        decay, piece = forward_part(got_ref[here], share)
        state_f = decay * state_f + piece
        other = member(blocks - 1 - block, L_ORDER)
        back_ref[other, share:] = state_b.astype(BF16)
        decay, piece = backward_part(got_ref[other], share)
        state_b = decay * state_b + piece


def final_kernel(state_ref, out_ref, reach_ref, y_ref, mixed_ref):
    owners, rows, _ = state_ref.shape
    share, heads = rows // 2, reach_ref.shape[1] // 2
    places = [member(owner, L_ORDER) for owner in range(owners)]
    ahead = jnp.concatenate([state_ref[place, :share] for place in places], axis=0)
    behind = jnp.concatenate([state_ref[place, share:] for place in places], axis=0)
    far_f = dot(out_ref[:, :STATE], ahead, LAST)
    far_b = dot(out_ref[:, STATE:], behind, LAST)
    reach = reach_ref[...]
    left = iota((SPAN, 2 * HEADDIM), 1) < HEADDIM
    for pair in range(heads // 2):
        here = slice(2 * HEADDIM * pair, 2 * HEADDIM * (pair + 1))
        h, g = 2 * pair, 2 * pair + heads
        scale_f = jnp.where(left, reach[:, h : h + 1], reach[:, h + 1 : h + 2])
        scale_b = jnp.where(left, reach[:, g : g + 1], reach[:, g + 1 : g + 2])
        mixed_ref[:, here] = (y_ref[:, here] + scale_f * far_f[:, here] + scale_b * far_b[:, here]).astype(BF16)


def call(kernel, out_shape, flops, **kwargs):
    return pl.pallas_call(
        kernel,
        out_shape=out_shape,
        compiler_params=pltpu.CompilerParams(vmem_limit_bytes=24 * 1024 * 1024),
        cost_estimate=pl.CostEstimate(flops=flops, bytes_accessed=1 << 20, transcendentals=0),
        **kwargs,
    )


def shards(hidden_in, w_inner, w_inout, w_step, step_bias, decay_rate, skip_gain):
    heads = w_step.shape[2]
    width = w_inner.shape[1]
    groups = lax.axis_size("zgroup")
    owners = lax.axis_size("zpart") * lax.axis_size("x")
    share = width // owners
    shape = jax.ShapeDtypeStruct
    copies = jnp.broadcast_to(hidden_in[None], (lax.axis_size("y"), *hidden_in.shape))
    x = lax.all_gather(exchange(copies, ("y",), Y_ORDER), "core", axis=0)
    sources = (w_step.transpose(0, 2, 1), step_bias, decay_rate, skip_gain, w_inout, w_inner)
    sources = tuple(pltpu.with_memory_space_constraint(a, pltpu.HBM) for a in sources)
    send, near, outs, reach = pl.pallas_call(
        local_kernel,
        out_shape=(
            shape((owners, 2 * share + EXTRA, STATE), BF16),
            shape((SPAN, width), F32),
            shape((SPAN, 2 * STATE), BF16),
            shape((SPAN, 2 * heads), F32),
        ),
        in_specs=[VMEM] + [HBM] * len(sources),
        out_specs=(VMEM,) * 4,
        scratch_shapes=[pltpu.VMEM(a.shape, a.dtype) for a in sources]
        + [pltpu.SemaphoreType.DMA((CUTS * len(sources),))],
        compiler_params=pltpu.CompilerParams(vmem_limit_bytes=24 * 1024 * 1024),
        cost_estimate=pl.CostEstimate(flops=700_000_000, bytes_accessed=6 << 20, transcendentals=0),
    )(x, *sources)
    got = exchange(send, ("zpart", "x"), L_ORDER)
    totals = call(total_kernel, shape((groups, share + EXTRA, STATE), BF16), 1_000_000)(got)
    totals = exchange(totals, ("zgroup",), Z_ORDER)
    back = call(scan_kernel, shape((owners, 2 * share, STATE), BF16), 1_000_000)(totals, got)
    state = exchange(back, ("zpart", "x"), L_ORDER)
    return call(final_kernel, shape((SPAN, width), BF16), 40_000_000)(state, outs, reach, near)


def solution(mesh):
    seq, head = mesh.shape["seq"], mesh.shape["head"]
    names = ("zgroup", "zpart", "x", "y", "core")
    fine = Mesh(mesh.devices.reshape(seq // (4 * DEPTH), DEPTH, 4, head // 2, 2), names)
    long, wide = ("zgroup", "zpart", "x"), ("y", "core")
    placed = (
        P((*long, *wide), None),
        P(None, wide),
        P(),
        P(None, None, wide),
        P(None, wide),
        P(wide),
        P(wide),
    )
    return jax.shard_map(
        shards, mesh=fine, in_specs=placed, out_specs=P(long, wide), check_vma=False
    )
```
